128 devices in a mesh: grp: 16 (over x, y), tp: 8 (over z, core).
Axes of the slice: x: 4, y: 4, z: 4, core: 2. Of those that a mesh axis runs over, the one named last changes fastest.
Arguments:
- queries: bfloat16 [32, 64, 256, 128], P('grp', 'tp'), may hold values from -8 to 8
- new_kv: bfloat16 [32, 8, 256, 256], P('grp', 'tp'), may hold values from -4.5 to 4.5
- kv_pool: bfloat16 [2048, 8, 128, 256], P(('grp', 'tp')), may hold values from -4.5 to 4.5
- cache_lens: int32 [32], replicated, may hold values from 1 to 7936, 126976 in all
- session_seat: int32 [32], replicated, may hold values from 0 to 31, as said below
- old_slots: int32 [32, 64], replicated, may hold values from 0 to 2047, as said below
- new_slots: int32 [32, 64], replicated, may hold values from 0 to 2047, as said below
Outputs:
- attention: bfloat16 [32, 64, 256, 128], P('grp', 'tp')
- new_pool: bfloat16 [2048, 8, 128, 256], P(('grp', 'tp'))
The draws below stay inside these ranges and needn't reach their ends.
Inputs may be any that keep to these rules, and one draw needn't show every extreme that they name: `session_seat`: A permutation of the sessions. `old_slots`: every pool block appears exactly once. Call the group of session s session_seat[s] // 2; every device of grp+tp holds exactly 1 of its 16 blocks for the sessions of each group. `new_slots`: every pool block appears exactly once, and every device holds exactly 1 block for the sessions of each group, as for old_slots.
All inputs are finite; a program needn't handle non-finite values.
Results may differ from the reference program's by a relative error of at most 0.005.
Values may be sent and summed in bfloat16 or wider, within the bound.
No kernel may reach another device: no remote copies, remote signals or barrier semaphores. Data moves between devices by JAX's collectives and lax.ppermute only.
A program may use at most 128 MiB of HBM per device.

```python
import math
import jax
import jax.numpy as jnp
import numpy as np
from jax import lax

QH = 64
KVH = 8
HD = 128
BLK = 128
MAXBLK = 64
TURN = 256
SPG = 2
SESS = 32
MAXLEN = 7936
SLOTS = 2048
POOL_DEV = 16


def seat_order(key):
    return jax.random.permutation(jax.random.fold_in(key, 101), SESS).astype(jnp.int32)


def slot_table(key, seat_of_session):
    owners = SESS * MAXBLK // POOL_DEV
    groups = SESS // SPG
    group_share = POOL_DEV // groups
    local_key, group_key = jax.random.split(key)
    local_codes = jax.vmap(lambda subkey: jax.random.permutation(subkey, POOL_DEV))(jax.random.split(local_key, owners))
    local_slot = jnp.argsort(local_codes, axis=1, stable=True).astype(jnp.int32)
    group_codes = jax.vmap(lambda subkey: jax.random.permutation(subkey, SPG * MAXBLK))(jax.random.split(group_key, groups))
    item_of = jnp.argsort(group_codes, axis=1, stable=True).astype(jnp.int32)
    seat_ids = jnp.arange(SESS, dtype=jnp.int32)[:, None]
    block_ids = jnp.arange(MAXBLK, dtype=jnp.int32)[None, :]
    group_of = seat_ids // SPG + 0 * block_ids
    position = seat_ids % SPG * MAXBLK + block_ids
    item = item_of[group_of, position]
    owner = item // group_share
    rank_in = item % group_share
    local = local_slot[owner, group_of * group_share + rank_in]
    by_seat = owner * POOL_DEV + local
    return by_seat[seat_of_session].astype(jnp.int32)


def draw_session_seat(key, part):
    return seat_order(key)


def draw_old_slots(key, part):
    seats = seat_order(key)
    key = jax.random.fold_in(key, 3)
    return slot_table(key, seats)


def draw_new_slots(key, part):
    seats = seat_order(key)
    key = jax.random.fold_in(key, 4)
    return slot_table(key, seats)


def draw_queries(key, part):
    key = jax.random.fold_in(key, 5)
    values = jnp.clip(2.0 * jax.random.normal(key, (SESS, QH, TURN, HD), jnp.float32), -8.0, 8.0)
    return values.astype(jnp.bfloat16)


def draw_new_kv(key, part):
    key = jax.random.fold_in(key, 6)
    values = jnp.clip(jax.random.normal(key, (SESS, KVH, TURN, 2 * HD), jnp.float32), -4.5, 4.5)
    return values.astype(jnp.bfloat16)


def level_of(own_key, shape, pieces, low, high):
    def one(axis_at, parts):
        steps = jax.random.uniform(jax.random.fold_in(jax.random.fold_in(own_key, 6), axis_at), (parts,), jnp.float32, low / len(pieces), high / len(pieces))
        return jnp.repeat(jnp.exp(steps), shape[axis_at] // parts).reshape((-1,) + (1,) * (len(shape) - axis_at - 1))

    level = one(*pieces[0])
    for cut in pieces[1:]:
        level = level * one(*cut)
    return level


def length_profile(number_of, total, limit, lean):
    loads = [(1 << 20) // math.isqrt(grade ** lean) + 1 for grade in range(2, number_of + 1)]
    spare, given = total - limit - (number_of - 1), [1] * (number_of - 1)
    while spare > 0:
        candidates = [i for i in range(number_of - 1) if given[i] < limit]
        whole, left = sum([loads[i] for i in candidates]), spare
        for i in candidates:
            more = min(limit - given[i], max(1, left * loads[i] // whole), spare)
            given[i] = given[i] + more
            spare = spare - more
    return np.array([limit] + given)


def ragged(own_key, count, total, most, slope):
    if count == 2:
        one = jax.random.randint(own_key, (), max(1, total - most), min(most, total - 1) + 1)
        return jnp.stack([one, total - one])
    lengths = jnp.asarray(length_profile(count, total, most, slope), jnp.int32)
    pairs = (count - 1) // 2
    source_of, sink = lengths[1:1 + 2 * pairs:2], lengths[2:2 + 2 * pairs:2]
    margin = jnp.minimum(source_of - 1, most - sink)
    moved = jax.random.randint(jax.random.fold_in(own_key, 1), (pairs,), 0, 1 << 20) % (margin + 1)
    lengths = lengths.at[1:1 + 2 * pairs:2].set(source_of - moved).at[2:2 + 2 * pairs:2].set(sink + moved)
    return lengths[jax.random.permutation(jax.random.fold_in(own_key, 2), count)]


def normal_values(own_key, extent, scale, bound, pieces=(), kind=jnp.bfloat16):
    entries = scale * jax.random.normal(own_key, extent, jnp.float32)
    if pieces:
        entries = entries * level_of(own_key, extent, pieces, -0.22, 0.18)
    return jnp.clip(entries, -bound, bound).astype(kind)


def setup_inputs(seed: int = 0) -> dict:
    keys = jax.random.split(jax.random.key(seed), 8)
    return {
        "queries": draw_queries(jax.random.fold_in(keys[7], 71), 0),
        "new_kv": draw_new_kv(jax.random.fold_in(keys[7], 71), 0),
        "kv_pool": normal_values(keys[2], (SLOTS, KVH, BLK, 2 * HD), 1.0, 4.5, ((0, 128),)),
        "cache_lens": ragged(keys[3], SESS, SESS * MAXLEN // 2, MAXLEN, 2).astype(jnp.int32),
        "session_seat": draw_session_seat(jax.random.fold_in(keys[7], 71), 0),
        "old_slots": draw_old_slots(jax.random.fold_in(keys[7], 71), 0),
        "new_slots": draw_new_slots(jax.random.fold_in(keys[7], 71), 0),
    }


def reference(queries, new_kv, kv_pool, cache_lens, session_seat, old_slots, new_slots):
    seat_session = jnp.zeros((SESS,), jnp.int32).at[session_seat].set(jnp.arange(SESS, dtype=jnp.int32))
    seat_lens = cache_lens[seat_session].astype(jnp.int32)
    old_table = old_slots[seat_session]
    new_table = new_slots[seat_session]
    key_span = MAXBLK * BLK
    group_size = QH // KVH

    def restore(inputs):
        table_row, length, fresh_kv = inputs
        blocks = kv_pool[table_row]
        cached = jnp.transpose(blocks, (1, 0, 2, 3)).reshape(KVH, key_span, 2 * HD)
        position = jnp.arange(key_span, dtype=jnp.int32)
        cached = jnp.where(position[None, :, None] < length, cached, jnp.zeros((), cached.dtype))
        zero_index = jnp.zeros((), jnp.int32)
        return lax.dynamic_update_slice(cached, fresh_kv, (zero_index, length.astype(jnp.int32), zero_index))

    grown_cache = lax.map(restore, (old_table, seat_lens, new_kv))

    def attend_seat(inputs):
        seat_queries, seat_grown, length = inputs
        turn_index = jnp.arange(group_size * TURN, dtype=jnp.int32) % TURN
        limits = length + turn_index
        column = jnp.arange(key_span, dtype=jnp.int32)

        def attend_head(head_inputs):
            head_queries, head_grown = head_inputs
            query_rows = head_queries.reshape(group_size * TURN, HD)
            scores = jnp.dot(query_rows, head_grown[:, :HD].T, preferred_element_type=jnp.float32) * (HD ** -0.5)
            scores = jnp.where(column[None, :] <= limits[:, None], scores, -1e30)
            highest = jnp.max(scores, axis=1, keepdims=True)
            weights = jnp.exp(scores - highest)
            weights = (weights / jnp.sum(weights, axis=1, keepdims=True)).astype(jnp.bfloat16)
            summed = jnp.dot(weights, head_grown[:, HD:], preferred_element_type=jnp.float32)
            return summed.astype(jnp.bfloat16).reshape(group_size, TURN, HD)

        return lax.map(attend_head, (seat_queries.reshape(KVH, group_size, TURN, HD), seat_grown))

    attention = lax.map(attend_seat, (queries, grown_cache, seat_lens)).reshape(SESS, QH, TURN, HD)
    grown_blocks = grown_cache.reshape(SESS, KVH, MAXBLK, BLK, 2 * HD)
    grown_blocks = jnp.transpose(grown_blocks, (0, 2, 1, 3, 4)).reshape(SESS * MAXBLK, KVH, BLK, 2 * HD)
    new_pool = jnp.zeros((SLOTS, KVH, BLK, 2 * HD), jnp.bfloat16).at[new_table.reshape(-1)].set(grown_blocks)
    return attention, new_pool
```

```python
import functools
import math

import jax
import jax.numpy as jnp
from jax import lax
from jax.experimental import pallas as pl
from jax.experimental.pallas import tpu as pltpu
from jax.sharding import PartitionSpec as P

MASKED = -1e30
CHUNK_BLOCKS = 8


def pack_kernel(code_ref, pool_ref, out_ref, sems):
    count = out_ref.shape[0]

    def copy(g):
        slot = code_ref[g] & (count - 1)
        return pltpu.make_async_copy(pool_ref.at[slot], out_ref.at[g], sems.at[g])

    for g in range(count):
        pl.when(code_ref[g] >= count)(lambda g=g: copy(g).start())
    for g in range(count):
        pl.when(code_ref[g] >= count)(lambda g=g: copy(g).wait())


def unpack_kernel(code_ref, arrived_ref, out_ref, zeros, sems):
    count = out_ref.shape[0]
    zeros[...] = jnp.zeros_like(zeros)

    def copy(g, live):
        slot = code_ref[g] & (count - 1)
        source = arrived_ref.at[g] if live else zeros
        return pltpu.make_async_copy(source, out_ref.at[slot], sems.at[g])

    for g in range(count):
        live = code_ref[g] >= count
        pl.when(live)(lambda g=g: copy(g, True).start())
        pl.when(jnp.logical_not(live))(lambda g=g: copy(g, False).start())
    for g in range(count):
        copy(g, False).wait()


def grow_kernel(
    src_ref, dst_ref, lens_ref, fresh_ref, recv_ref, out_ref, edge_in, edge_out, sems, edge_sems
):
    seats, max_blocks = src_ref.shape
    block_len = recv_ref.shape[1]
    turn = fresh_ref.shape[1]
    spill = turn // block_len + 1

    def row_copy(q, j):
        return pltpu.make_async_copy(
            recv_ref.at[src_ref[q, j]], out_ref.at[dst_ref[q, j]], sems.at[q, j]
        )

    def edge_load(q):
        edge = lens_ref[q] // block_len
        return pltpu.make_async_copy(recv_ref.at[src_ref[q, edge]], edge_in.at[q], edge_sems.at[q, 0])

    def edge_store(q, k):
        edge = lens_ref[q] // block_len
        return pltpu.make_async_copy(
            edge_out.at[q, pl.ds(k * block_len, block_len)],
            out_ref.at[dst_ref[q, edge + k]],
            edge_sems.at[q, 1 + k],
        )

    for q in range(seats):
        edge_load(q).start()
    for q in range(seats):
        pl.loop(0, lens_ref[q] // block_len)(lambda j, q=q: row_copy(q, j).start())
    for q in range(seats):
        rest = lens_ref[q] % block_len
        fresh = fresh_ref[q].astype(jnp.float32)
        tail = jnp.zeros((block_len, fresh.shape[1]), jnp.float32)
        moved = pltpu.roll(jnp.concatenate([fresh, tail], axis=0), rest, 0)
        edge_load(q).wait()
        row = lax.broadcasted_iota(jnp.int32, (block_len, fresh.shape[1]), 0)
        first = jnp.where(row < rest, edge_in[q].astype(jnp.float32), moved[:block_len])
        edge_out[q, :block_len] = first.astype(edge_out.dtype)
        edge_out[q, block_len:] = moved[block_len:].astype(edge_out.dtype)
        for k in range(spill - 1):
            edge_store(q, k).start()
        pl.when(rest > 0)(lambda q=q: edge_store(q, spill - 1).start())
    for q in range(seats):
        for k in range(spill - 1):
            edge_store(q, k).wait()
        rest = lens_ref[q] % block_len
        pl.when(rest > 0)(lambda q=q: edge_store(q, spill - 1).wait())
    for q in range(seats):
        pl.loop(0, lens_ref[q] // block_len)(lambda j, q=q: row_copy(q, j).wait())


def attend_kernel(
    src_ref, lens_ref, queries_ref, fresh_ref, recv_ref, out_ref, cache, acc, high, sems
):
    seats, max_blocks = src_ref.shape
    block_len = recv_ref.shape[1]
    head_dim = queries_ref.shape[3]
    heads = queries_ref.shape[1]
    turn = queries_ref.shape[2]
    span = CHUNK_BLOCKS * block_len
    factor = head_dim ** (-0.5) * math.log2(math.e)
    pair = 2

    def row_copy(q, j):
        return pltpu.make_async_copy(
            recv_ref.at[src_ref[q, j]],
            cache.at[q, pl.ds(pl.multiple_of(j * block_len, block_len), block_len)],
            sems.at[q, j],
        )

    def blocks_of(q):
        return (lens_ref[q] + block_len - 1) // block_len

    def chunks_of(q):
        return (lens_ref[q] + span - 1) // span

    for q in range(seats):
        pl.loop(0, blocks_of(q))(lambda j, q=q: row_copy(q, j).start())

    def values_of(rows):
        ones = jnp.ones((rows.shape[0], head_dim), rows.dtype)
        return jnp.concatenate([rows[:, head_dim:], ones], axis=1)

    def score(query, rows):
        return (
            lax.dot_general(
                query, rows[:, :head_dim], (((1,), (1,)), ((), ())),
                preferred_element_type=jnp.float32,
            )
            * factor
        )

    def weigh(scores, top, rows):
        weights = jnp.exp2(scores - top).astype(jnp.bfloat16)
        return jnp.dot(weights, values_of(rows), preferred_element_type=jnp.float32)

    for q in range(seats):
        length = lens_ref[q]
        pl.loop(0, blocks_of(q))(lambda j, q=q: row_copy(q, j).wait())

        @pl.loop(blocks_of(q), chunks_of(q) * CHUNK_BLOCKS)
        def _(j, q=q):
            start = pl.multiple_of(j * block_len, block_len)
            cache[q, pl.ds(start, block_len)] = jnp.zeros((block_len, cache.shape[2]), cache.dtype)

        @pl.loop(0, heads // pair)
        def _(h, q=q, length=length):
            row = lax.broadcasted_iota(jnp.int32, (turn, turn), 0)
            column = lax.broadcasted_iota(jnp.int32, (turn, turn), 1)
            fresh = fresh_ref[q]
            for k in range(pair):
                scores = score(queries_ref[q, h * pair + k], fresh)
                scores = jnp.where(column <= row, scores, MASKED)
                top = jnp.max(scores, axis=1, keepdims=True)
                acc[k] = weigh(scores, top, fresh)
                high[k] = jnp.broadcast_to(top, high.shape[1:])

            def step(c, masked):
                start = pl.multiple_of(c * span, span)
                rows = cache[q, pl.ds(start, span)]
                for k in range(pair):
                    scores = score(queries_ref[q, h * pair + k], rows)
                    if masked:
                        position = start + lax.broadcasted_iota(jnp.int32, (1, span), 1)
                        scores = jnp.where(position < length, scores, MASKED)
                    old = high[k, :, :1]
                    top = jnp.maximum(old, jnp.max(scores, axis=1, keepdims=True))
                    acc[k] = acc[k] * jnp.exp2(old - top) + weigh(scores, top, rows)
                    high[k] = jnp.broadcast_to(top, high.shape[1:])

            full = length // span
            pl.loop(0, full)(lambda c: step(c, False))
            pl.when(length > full * span)(lambda: step(full, True))
            for k in range(pair):
                total = acc[k, :, head_dim : head_dim + 1]
                out_ref[q, h * pair + k] = (acc[k, :, :head_dim] / total).astype(out_ref.dtype)


def local(queries, new_kv, kv_pool, cache_lens, session_seat, old_slots, new_slots):
    group_count = lax.axis_size("grp")
    tp_count = lax.axis_size("tp")
    pool_dev, kv_heads, block_len, pair_width = kv_pool.shape
    seats_group, heads, turn, head_dim = queries.shape
    max_blocks = old_slots.shape[1]
    owners = group_count * tp_count
    assert pool_dev == group_count and kv_heads == tp_count
    group_index = lax.axis_index("grp")
    my_index = group_index * tp_count + lax.axis_index("tp")
    dtype = kv_pool.dtype
    any_space = pl.BlockSpec(memory_space=pl.ANY)
    vmem = pl.BlockSpec(memory_space=pltpu.VMEM)

    block_start = jnp.arange(max_blocks, dtype=jnp.int32)[None, :] * block_len
    session_group = session_seat // seats_group
    group_ids = jnp.arange(group_count, dtype=jnp.int32)

    def codes(slots, lengths):
        live = (block_start < lengths[:, None]).astype(jnp.int32)
        code = slots % pool_dev + pool_dev * live
        code = jnp.where(slots // pool_dev == my_index, code, 0)
        picked = jnp.where(session_group[None, :, None] == group_ids[:, None, None], code[None], 0)
        return jnp.sum(picked, axis=(1, 2))

    pack_codes = codes(old_slots, cache_lens)
    outgoing = pl.pallas_call(
        pack_kernel,
        grid_spec=pltpu.PrefetchScalarGridSpec(
            num_scalar_prefetch=1,
            grid=(1,),
            in_specs=[any_space],
            out_specs=any_space,
            scratch_shapes=[pltpu.SemaphoreType.DMA((group_count,))],
        ),
        out_shape=jax.ShapeDtypeStruct((group_count, kv_heads, block_len, pair_width), dtype),
        name="pack",
    )(pack_codes, kv_pool)
    received = lax.all_to_all(
        outgoing.reshape(owners, block_len, pair_width),
        ("grp", "tp"), split_axis=0, concat_axis=0, tiled=True,
    )

    seat_ids = group_index * seats_group + jnp.arange(seats_group, dtype=jnp.int32)
    mine = (session_seat[None, :] == seat_ids[:, None]).astype(jnp.int32)
    my_lens = jnp.sum(mine * cache_lens[None, :], axis=1)
    my_old = jnp.sum(mine[:, :, None] * (old_slots // pool_dev)[None], axis=1)
    my_new = jnp.sum(mine[:, :, None] * (new_slots // pool_dev)[None], axis=1)
    unpack_codes = codes(new_slots, cache_lens + turn)
    fresh = new_kv.reshape(seats_group, turn, pair_width)

    spill = turn // block_len + 1
    leaving = pl.pallas_call(
        grow_kernel,
        grid_spec=pltpu.PrefetchScalarGridSpec(
            num_scalar_prefetch=3,
            grid=(1,),
            in_specs=[vmem, any_space],
            out_specs=any_space,
            scratch_shapes=[
                pltpu.VMEM((seats_group, block_len, pair_width), dtype),
                pltpu.VMEM((seats_group, spill * block_len, pair_width), dtype),
                pltpu.SemaphoreType.DMA((seats_group, max_blocks)),
                pltpu.SemaphoreType.DMA((seats_group, 1 + spill)),
            ],
        ),
        out_shape=jax.ShapeDtypeStruct((owners, block_len, pair_width), dtype),
        name="grow",
    )(my_old, my_new, my_lens, fresh, received)
    arrived = lax.all_to_all(leaving, ("grp", "tp"), split_axis=0, concat_axis=0, tiled=True)

    attention = pl.pallas_call(
        attend_kernel,
        grid_spec=pltpu.PrefetchScalarGridSpec(
            num_scalar_prefetch=2,
            grid=(1,),
            in_specs=[vmem, vmem, any_space],
            out_specs=vmem,
            scratch_shapes=[
                pltpu.VMEM((seats_group, max_blocks * block_len, pair_width), dtype),
                pltpu.VMEM((2, turn, 2 * head_dim), jnp.float32),
                pltpu.VMEM((2, turn, head_dim), jnp.float32),
                pltpu.SemaphoreType.DMA((seats_group, max_blocks)),
            ],
        ),
        out_shape=jax.ShapeDtypeStruct(queries.shape, dtype),
        compiler_params=pltpu.CompilerParams(vmem_limit_bytes=40 * 1024 * 1024),
        cost_estimate=pl.CostEstimate(
            flops=4 * seats_group * heads * turn * max_blocks * block_len * head_dim,
            bytes_accessed=owners * block_len * pair_width * 2,
            transcendentals=seats_group * heads * turn * max_blocks * block_len,
        ),
        name="attend",
    )(my_old, my_lens, queries, fresh, received)

    new_pool = pl.pallas_call(
        unpack_kernel,
        grid_spec=pltpu.PrefetchScalarGridSpec(
            num_scalar_prefetch=1,
            grid=(1,),
            in_specs=[any_space],
            out_specs=any_space,
            scratch_shapes=[
                pltpu.VMEM((kv_heads, block_len, pair_width), dtype),
                pltpu.SemaphoreType.DMA((group_count,)),
            ],
        ),
        out_shape=jax.ShapeDtypeStruct(kv_pool.shape, dtype),
        name="unpack",
    )(unpack_codes, arrived.reshape(group_count, kv_heads, block_len, pair_width))
    return attention, new_pool


def solution(mesh):
    in_specs = (
        P("grp", "tp", None, None),
        P("grp", "tp", None, None),
        P(("grp", "tp"), None, None, None),
        P(),
        P(),
        P(),
        P(),
    )
    out_specs = (P("grp", "tp", None, None), P(("grp", "tp"), None, None, None))
    return jax.shard_map(local, mesh=mesh, in_specs=in_specs, out_specs=out_specs, check_vma=False)
```

```python
import functools
import math

import jax
import jax.numpy as jnp
from jax import lax
from jax.experimental import pallas as pl
from jax.experimental.pallas import tpu as pltpu
from jax.sharding import PartitionSpec as P

MASKED = -1e30
CHUNK_BLOCKS = 8


def pack_kernel(code_ref, pool_ref, out_ref, held, load_sems, store_sems):
    count = out_ref.shape[0]

    def load(g):
        slot = lax.rem(code_ref[g], count)
        return pltpu.make_async_copy(pool_ref.at[slot], held.at[g], load_sems.at[g])

    def store(g):
        return pltpu.make_async_copy(held.at[g], out_ref.at[g], store_sems.at[g])

    def forward(g):
        load(g).wait()
        store(g).start()

    for g in range(count):
        pl.when(code_ref[g] >= count)(lambda g=g: load(g).start())
    for g in range(count):
        pl.when(code_ref[g] >= count)(lambda g=g: forward(g))
    for g in range(count):
        pl.when(code_ref[g] >= count)(lambda g=g: store(g).wait())


def unpack_kernel(code_ref, arrived_ref, out_ref, held, zeros, load_sems, store_sems):
    count = out_ref.shape[0]

    def load(g):
        return pltpu.make_async_copy(arrived_ref.at[g], held.at[g], load_sems.at[g])

    def store(g, source):
        slot = lax.rem(code_ref[g], count)
        return pltpu.make_async_copy(source, out_ref.at[slot], store_sems.at[g])

    def forward(g):
        load(g).wait()
        store(g, held.at[g]).start()

    for g in range(count):
        pl.when(code_ref[g] >= count)(lambda g=g: load(g).start())
    zeros[...] = jnp.zeros_like(zeros)
    for g in range(count):
        pl.when(code_ref[g] < count)(lambda g=g: store(g, zeros).start())
    for g in range(count):
        pl.when(code_ref[g] >= count)(lambda g=g: forward(g))
    for g in range(count):
        store(g, zeros).wait()


def grow_kernel(
    src_ref, dst_ref, lens_ref, fresh_ref, recv_ref, out_ref,
    held, edge_in, edge_out, load_sems, store_sems, edge_sems,
):
    seats, max_blocks = src_ref.shape
    block_len = recv_ref.shape[1]
    turn = fresh_ref.shape[1]
    spill = turn // block_len + 1

    def load(q, j):
        return pltpu.make_async_copy(recv_ref.at[src_ref[q, j]], held.at[q, j], load_sems.at[q, j])

    def store(q, j):
        return pltpu.make_async_copy(held.at[q, j], out_ref.at[dst_ref[q, j]], store_sems.at[q, j])

    def forward(q, j):
        load(q, j).wait()
        store(q, j).start()

    def edge_load(q):
        edge = lens_ref[q] // block_len
        return pltpu.make_async_copy(recv_ref.at[src_ref[q, edge]], edge_in.at[q], edge_sems.at[q, 0])

    def edge_store(q, k):
        edge = lens_ref[q] // block_len
        return pltpu.make_async_copy(
            edge_out.at[q, pl.ds(k * block_len, block_len)],
            out_ref.at[dst_ref[q, edge + k]],
            edge_sems.at[q, 1 + k],
        )

    for q in range(seats):
        edge_load(q).start()
    for q in range(seats):
        pl.loop(0, lens_ref[q] // block_len)(lambda j, q=q: load(q, j).start())
    for q in range(seats):
        pl.loop(0, lens_ref[q] // block_len)(lambda j, q=q: forward(q, j))
    for q in range(seats):
        rest = lens_ref[q] % block_len
        fresh = fresh_ref[q].astype(jnp.float32)
        tail = jnp.zeros((block_len, fresh.shape[1]), jnp.float32)
        moved = pltpu.roll(jnp.concatenate([fresh, tail], axis=0), rest, 0)
        edge_load(q).wait()
        row = lax.broadcasted_iota(jnp.int32, (block_len, fresh.shape[1]), 0)
        first = jnp.where(row < rest, edge_in[q].astype(jnp.float32), moved[:block_len])
        edge_out[q, :block_len] = first.astype(edge_out.dtype)
        edge_out[q, block_len:] = moved[block_len:].astype(edge_out.dtype)
        for k in range(spill - 1):
            edge_store(q, k).start()
        pl.when(rest > 0)(lambda q=q: edge_store(q, spill - 1).start())
    for q in range(seats):
        for k in range(spill - 1):
            edge_store(q, k).wait()
        rest = lens_ref[q] % block_len
        pl.when(rest > 0)(lambda q=q: edge_store(q, spill - 1).wait())
    for q in range(seats):
        pl.loop(0, lens_ref[q] // block_len)(lambda j, q=q: store(q, j).wait())


def attend_kernel(
    src_ref, lens_ref, queries_ref, fresh_ref, recv_ref, out_ref, cache, acc, high, sems
):
    seats, max_blocks = src_ref.shape
    block_len = recv_ref.shape[1]
    head_dim = queries_ref.shape[3]
    heads = queries_ref.shape[1]
    turn = queries_ref.shape[2]
    span = CHUNK_BLOCKS * block_len
    factor = head_dim ** (-0.5) * math.log2(math.e)
    pair = 2

    def row_copy(q, j):
        return pltpu.make_async_copy(
            recv_ref.at[src_ref[q, j]],
            cache.at[q, pl.ds(pl.multiple_of(j * block_len, block_len), block_len)],
            sems.at[q, j],
        )

    def blocks_of(q):
        return (lens_ref[q] + block_len - 1) // block_len

    def chunks_of(q):
        return (lens_ref[q] + span - 1) // span

    for q in range(seats):
        pl.loop(0, blocks_of(q))(lambda j, q=q: row_copy(q, j).start())

    def values_of(rows):
        ones = jnp.ones((rows.shape[0], head_dim), rows.dtype)
        return jnp.concatenate([rows[:, head_dim:], ones], axis=1)

    def score(query, rows):
        return (
            lax.dot_general(
                query, rows[:, :head_dim], (((1,), (1,)), ((), ())),
                preferred_element_type=jnp.float32,
            )
            * factor
        )

    def weigh(scores, top, rows):
        weights = jnp.exp2(scores - top).astype(jnp.bfloat16)
        return jnp.dot(weights, values_of(rows), preferred_element_type=jnp.float32)

    for q in range(seats):
        length = lens_ref[q]
        pl.loop(0, blocks_of(q))(lambda j, q=q: row_copy(q, j).wait())

        @pl.loop(blocks_of(q), chunks_of(q) * CHUNK_BLOCKS)
        def _(j, q=q):
            start = pl.multiple_of(j * block_len, block_len)
            cache[q, pl.ds(start, block_len)] = jnp.zeros((block_len, cache.shape[2]), cache.dtype)

        @pl.loop(0, heads // pair)
        def _(h, q=q, length=length):
            row = lax.broadcasted_iota(jnp.int32, (turn, turn), 0)
            column = lax.broadcasted_iota(jnp.int32, (turn, turn), 1)
            fresh = fresh_ref[q]
            for k in range(pair):
                scores = score(queries_ref[q, h * pair + k], fresh)
                scores = jnp.where(column <= row, scores, MASKED)
                top = jnp.max(scores, axis=1, keepdims=True)
                acc[k] = weigh(scores, top, fresh)
                high[k] = jnp.broadcast_to(top, high.shape[1:])

            def step(c, masked):
                start = pl.multiple_of(c * span, span)
                rows = cache[q, pl.ds(start, span)]
                for k in range(pair):
                    scores = score(queries_ref[q, h * pair + k], rows)
                    if masked:
                        position = start + lax.broadcasted_iota(jnp.int32, (1, span), 1)
                        scores = jnp.where(position < length, scores, MASKED)
                    old = high[k, :, :1]
                    top = jnp.maximum(old, jnp.max(scores, axis=1, keepdims=True))
                    acc[k] = acc[k] * jnp.exp2(old - top) + weigh(scores, top, rows)
                    high[k] = jnp.broadcast_to(top, high.shape[1:])

            full = length // span
            pl.loop(0, full)(lambda c: step(c, False))
            pl.when(length > full * span)(lambda: step(full, True))
            for k in range(pair):
                total = acc[k, :, head_dim : head_dim + 1]
                out_ref[q, h * pair + k] = (acc[k, :, :head_dim] / total).astype(out_ref.dtype)


def local(queries, new_kv, kv_pool, cache_lens, session_seat, old_slots, new_slots):
    group_count = lax.axis_size("grp")
    tp_count = lax.axis_size("tp")
    pool_dev, kv_heads, block_len, pair_width = kv_pool.shape
    seats_group, heads, turn, head_dim = queries.shape
    max_blocks = old_slots.shape[1]
    owners = group_count * tp_count
    assert pool_dev == group_count and kv_heads == tp_count
    group_index = lax.axis_index("grp")
    my_index = group_index * tp_count + lax.axis_index("tp")
    dtype = kv_pool.dtype
    any_space = pl.BlockSpec(memory_space=pl.ANY)
    vmem = pl.BlockSpec(memory_space=pltpu.VMEM)

    block_start = jnp.arange(max_blocks, dtype=jnp.int32)[None, :] * block_len
    session_group = session_seat // seats_group
    group_ids = jnp.arange(group_count, dtype=jnp.int32)

    def codes(slots, lengths):
        live = (block_start < lengths[:, None]).astype(jnp.int32)
        code = slots % pool_dev + pool_dev * live
        code = jnp.where(slots // pool_dev == my_index, code, 0)
        picked = jnp.where(session_group[None, :, None] == group_ids[:, None, None], code[None], 0)
        return jnp.sum(picked, axis=(1, 2))

    pack_codes = codes(old_slots, cache_lens)
    outgoing = pl.pallas_call(
        pack_kernel,
        grid_spec=pltpu.PrefetchScalarGridSpec(
            num_scalar_prefetch=1,
            grid=(1,),
            in_specs=[any_space],
            out_specs=any_space,
            scratch_shapes=[
                pltpu.VMEM((group_count, kv_heads, block_len, pair_width), dtype),
                pltpu.SemaphoreType.DMA((group_count,)),
                pltpu.SemaphoreType.DMA((group_count,)),
            ],
        ),
        out_shape=jax.ShapeDtypeStruct((group_count, kv_heads, block_len, pair_width), dtype),
        compiler_params=pltpu.CompilerParams(vmem_limit_bytes=16 * 1024 * 1024),
        name="pack",
    )(pack_codes, kv_pool)
    received = lax.all_to_all(
        outgoing.reshape(owners, block_len, pair_width),
        ("grp", "tp"), split_axis=0, concat_axis=0, tiled=True,
    )

    seat_ids = group_index * seats_group + jnp.arange(seats_group, dtype=jnp.int32)
    mine = (session_seat[None, :] == seat_ids[:, None]).astype(jnp.int32)
    my_lens = jnp.sum(mine * cache_lens[None, :], axis=1)
    my_old = jnp.sum(mine[:, :, None] * (old_slots // pool_dev)[None], axis=1)
    my_new = jnp.sum(mine[:, :, None] * (new_slots // pool_dev)[None], axis=1)
    unpack_codes = codes(new_slots, cache_lens + turn)
    fresh = new_kv.reshape(seats_group, turn, pair_width)

    spill = turn // block_len + 1
    leaving = pl.pallas_call(
        grow_kernel,
        grid_spec=pltpu.PrefetchScalarGridSpec(
            num_scalar_prefetch=3,
            grid=(1,),
            in_specs=[vmem, any_space],
            out_specs=any_space,
            scratch_shapes=[
                pltpu.VMEM((seats_group, max_blocks, block_len, pair_width), dtype),
                pltpu.VMEM((seats_group, block_len, pair_width), dtype),
                pltpu.VMEM((seats_group, spill * block_len, pair_width), dtype),
                pltpu.SemaphoreType.DMA((seats_group, max_blocks)),
                pltpu.SemaphoreType.DMA((seats_group, max_blocks)),
                pltpu.SemaphoreType.DMA((seats_group, 1 + spill)),
            ],
        ),
        out_shape=jax.ShapeDtypeStruct((owners, block_len, pair_width), dtype),
        compiler_params=pltpu.CompilerParams(vmem_limit_bytes=20 * 1024 * 1024),
        name="grow",
    )(my_old, my_new, my_lens, fresh, received)
    arrived = lax.all_to_all(leaving, ("grp", "tp"), split_axis=0, concat_axis=0, tiled=True)

    attention = pl.pallas_call(
        attend_kernel,
        grid_spec=pltpu.PrefetchScalarGridSpec(
            num_scalar_prefetch=2,
            grid=(1,),
            in_specs=[vmem, vmem, any_space],
            out_specs=vmem,
            scratch_shapes=[
                pltpu.VMEM((seats_group, max_blocks * block_len, pair_width), dtype),
                pltpu.VMEM((2, turn, 2 * head_dim), jnp.float32),
                pltpu.VMEM((2, turn, head_dim), jnp.float32),
                pltpu.SemaphoreType.DMA((seats_group, max_blocks)),
            ],
        ),
        out_shape=jax.ShapeDtypeStruct(queries.shape, dtype),
        compiler_params=pltpu.CompilerParams(vmem_limit_bytes=40 * 1024 * 1024),
        cost_estimate=pl.CostEstimate(
            flops=4 * seats_group * heads * turn * max_blocks * block_len * head_dim,
            bytes_accessed=owners * block_len * pair_width * 2,
            transcendentals=seats_group * heads * turn * max_blocks * block_len,
        ),
        name="attend",
    )(my_old, my_lens, queries, fresh, received)

    new_pool = pl.pallas_call(
        unpack_kernel,
        grid_spec=pltpu.PrefetchScalarGridSpec(
            num_scalar_prefetch=1,
            grid=(1,),
            in_specs=[any_space],
            out_specs=any_space,
            scratch_shapes=[
                pltpu.VMEM((group_count, kv_heads, block_len, pair_width), dtype),
                pltpu.VMEM((kv_heads, block_len, pair_width), dtype),
                pltpu.SemaphoreType.DMA((group_count,)),
                pltpu.SemaphoreType.DMA((group_count,)),
            ],
        ),
        out_shape=jax.ShapeDtypeStruct(kv_pool.shape, dtype),
        compiler_params=pltpu.CompilerParams(vmem_limit_bytes=16 * 1024 * 1024),
        name="unpack",
    )(unpack_codes, arrived.reshape(group_count, kv_heads, block_len, pair_width))
    return attention, new_pool


def solution(mesh):
    in_specs = (
        P("grp", "tp", None, None),
        P("grp", "tp", None, None),
        P(("grp", "tp"), None, None, None),
        P(),
        P(),
        P(),
        P(),
    )
    out_specs = (P("grp", "tp", None, None), P(("grp", "tp"), None, None, None))
    return jax.shard_map(local, mesh=mesh, in_specs=in_specs, out_specs=out_specs, check_vma=False)
```

```python
import functools
import math

import jax
import jax.numpy as jnp
from jax import lax
from jax.experimental import pallas as pl
from jax.experimental.pallas import tpu as pltpu
from jax.sharding import PartitionSpec as P

MASKED = -1e30
CHUNK_BLOCKS = 8


def pack_kernel(slots_ref, seats_ref, lens_ref, pool_ref, out_ref, held, load_sems, store_sems, *, seats):
    count, tp_count, block_len = pool_ref.shape[:3]
    sessions, max_blocks = slots_ref.shape

    def load(i):
        return pltpu.make_async_copy(pool_ref.at[i], held.at[i], load_sems.at[i])

    def store(i, g):
        return pltpu.make_async_copy(held.at[i], out_ref.at[g], store_sems.at[i])

    for i in range(count):
        load(i).start()
    square = (sessions, sessions)
    diagonal = lax.broadcasted_iota(jnp.int32, square, 0) == lax.broadcasted_iota(jnp.int32, square, 1)

    def column(row):
        return jnp.sum(jnp.where(diagonal, row, 0), axis=1, keepdims=True)

    group = lax.div(column(seats_ref[...]), seats)
    start = lax.broadcasted_iota(jnp.int32, (sessions, max_blocks), 1) * block_len
    code = jnp.where(start < column(lens_ref[...]), group + 1, 0)
    my_index = lax.axis_index("grp") * tp_count + lax.axis_index("tp")
    slot = slots_ref[...] - my_index * count
    codes = [jnp.sum(jnp.where(slot == i, code, 0)) for i in range(count)]

    def forward(i):
        load(i).wait()
        pl.when(codes[i] > 0)(lambda: store(i, codes[i] - 1).start())

    for i in range(count):
        forward(i)
    for i in range(count):
        pl.when(codes[i] > 0)(lambda i=i: store(i, codes[i] - 1).wait())


def unpack_kernel(code_ref, arrived_ref, out_ref, held, zeros, load_sems, store_sems):
    count = out_ref.shape[0]

    def load(g):
        return pltpu.make_async_copy(arrived_ref.at[g], held.at[g], load_sems.at[g])

    def store(g, source):
        slot = lax.rem(code_ref[g], count)
        return pltpu.make_async_copy(source, out_ref.at[slot], store_sems.at[g])

    def forward(g):
        load(g).wait()
        store(g, held.at[g]).start()

    for g in range(count):
        pl.when(code_ref[g] >= count)(lambda g=g: load(g).start())
    zeros[...] = jnp.zeros_like(zeros)
    for g in range(count):
        pl.when(code_ref[g] < count)(lambda g=g: store(g, zeros).start())
    for g in range(count):
        pl.when(code_ref[g] >= count)(lambda g=g: forward(g))
    for g in range(count):
        store(g, zeros).wait()


def grow_kernel(
    pick_ref, dst_ref, edge_ref, lens_ref, fresh_ref, recv_ref, out_ref,
    held, edge_in, load_sems, store_sem, edge_sems,
):
    owners, block_len, width = recv_ref.shape
    seats, turn = fresh_ref.shape[:2]
    spill = turn // block_len + 1
    parts = load_sems.shape[0]
    share = owners // parts

    def load(c):
        rows = pl.ds(c * share, share)
        return pltpu.make_async_copy(recv_ref.at[rows], held.at[rows], load_sems.at[c])

    def edge_load(q):
        return pltpu.make_async_copy(recv_ref.at[edge_ref[q]], edge_in.at[q], edge_sems.at[q])

    for q in range(seats):
        edge_load(q).start()
    for c in range(parts):
        load(c).start()
    row = lax.broadcasted_iota(jnp.int32, (block_len, width), 0)
    for q in range(seats):
        rest = lax.rem(lens_ref[q], block_len)
        tail = jnp.zeros((block_len, width), jnp.float32)
        moved = jnp.concatenate([fresh_ref[q].astype(jnp.float32), tail], axis=0)
        moved = pltpu.roll(moved, rest, 0)
        edge_load(q).wait()
        first = jnp.where(row < rest, edge_in[q].astype(jnp.float32), moved[:block_len])
        held[owners + q * spill] = first.astype(held.dtype)
        for k in range(1, spill):
            later = moved[k * block_len : (k + 1) * block_len]
            held[owners + q * spill + k] = later.astype(held.dtype)
    for c in range(parts):
        load(c).wait()
        for o in range(c * share, (c + 1) * share):
            pltpu.make_async_copy(held.at[pick_ref[o]], out_ref.at[dst_ref[o]], store_sem).start()
    pltpu.make_async_copy(held.at[pl.ds(0, owners)], out_ref, store_sem).wait()


def attend_kernel(
    src_ref, lens_ref, queries_ref, fresh_ref, recv_ref, out_ref, cache, acc, high, sems
):
    seats, max_blocks = src_ref.shape
    block_len = recv_ref.shape[1]
    head_dim = queries_ref.shape[3]
    heads = queries_ref.shape[1]
    turn = queries_ref.shape[2]
    span = CHUNK_BLOCKS * block_len
    factor = head_dim ** (-0.5) * math.log2(math.e)
    pair = 2

    def row_copy(q, j):
        return pltpu.make_async_copy(
            recv_ref.at[src_ref[q, j]],
            cache.at[q, pl.ds(pl.multiple_of(j * block_len, block_len), block_len)],
            sems.at[q, j],
        )

    def blocks_of(q):
        return (lens_ref[q] + block_len - 1) // block_len

    def chunks_of(q):
        return (lens_ref[q] + span - 1) // span

    for q in range(seats):
        pl.loop(0, blocks_of(q))(lambda j, q=q: row_copy(q, j).start())

    def values_of(rows):
        ones = jnp.ones((rows.shape[0], head_dim), rows.dtype)
        return jnp.concatenate([rows[:, head_dim:], ones], axis=1)

    def score(query, rows):
        return (
            lax.dot_general(
                query, rows[:, :head_dim], (((1,), (1,)), ((), ())),
                preferred_element_type=jnp.float32,
            )
            * factor
        )

    def weigh(scores, top, rows):
        weights = jnp.exp2(scores - top).astype(jnp.bfloat16)
        return jnp.dot(weights, values_of(rows), preferred_element_type=jnp.float32)

    for q in range(seats):
        length = lens_ref[q]
        pl.loop(0, blocks_of(q))(lambda j, q=q: row_copy(q, j).wait())

        @pl.loop(blocks_of(q), chunks_of(q) * CHUNK_BLOCKS)
        def _(j, q=q):
            start = pl.multiple_of(j * block_len, block_len)
            cache[q, pl.ds(start, block_len)] = jnp.zeros((block_len, cache.shape[2]), cache.dtype)

        @pl.loop(0, heads // pair)
        def _(h, q=q, length=length):
            row = lax.broadcasted_iota(jnp.int32, (turn, turn), 0)
            column = lax.broadcasted_iota(jnp.int32, (turn, turn), 1)
            fresh = fresh_ref[q]
            for k in range(pair):
                scores = score(queries_ref[q, h * pair + k], fresh)
                scores = jnp.where(column <= row, scores, MASKED)
                top = jnp.max(scores, axis=1, keepdims=True)
                acc[k] = weigh(scores, top, fresh)
                high[k] = jnp.broadcast_to(top, high.shape[1:])

            def step(c, masked):
                start = pl.multiple_of(c * span, span)
                rows = cache[q, pl.ds(start, span)]
                for k in range(pair):
                    scores = score(queries_ref[q, h * pair + k], rows)
                    if masked:
                        position = start + lax.broadcasted_iota(jnp.int32, (1, span), 1)
                        scores = jnp.where(position < length, scores, MASKED)
                    old = high[k, :, :1]
                    top = jnp.maximum(old, jnp.max(scores, axis=1, keepdims=True))
                    acc[k] = acc[k] * jnp.exp2(old - top) + weigh(scores, top, rows)
                    high[k] = jnp.broadcast_to(top, high.shape[1:])

            full = length // span
            pl.loop(0, full)(lambda c: step(c, False))
            pl.when(length > full * span)(lambda: step(full, True))
            for k in range(pair):
                total = acc[k, :, head_dim : head_dim + 1]
                out_ref[q, h * pair + k] = (acc[k, :, :head_dim] / total).astype(out_ref.dtype)


def local(queries, new_kv, kv_pool, cache_lens, session_seat, old_slots, new_slots):
    group_count = lax.axis_size("grp")
    tp_count = lax.axis_size("tp")
    pool_dev, kv_heads, block_len, pair_width = kv_pool.shape
    seats_group, heads, turn, head_dim = queries.shape
    max_blocks = old_slots.shape[1]
    owners = group_count * tp_count
    assert pool_dev == group_count and kv_heads == tp_count
    group_index = lax.axis_index("grp")
    my_index = group_index * tp_count + lax.axis_index("tp")
    dtype = kv_pool.dtype
    hbm = pl.BlockSpec(memory_space=pltpu.HBM)
    vmem = pl.BlockSpec(memory_space=pltpu.VMEM)

    block_start = jnp.arange(max_blocks, dtype=jnp.int32)[None, :] * block_len
    session_group = session_seat // seats_group
    group_ids = jnp.arange(group_count, dtype=jnp.int32)

    def codes(slots, lengths):
        live = (block_start < lengths[:, None]).astype(jnp.int32)
        code = slots % pool_dev + pool_dev * live
        code = jnp.where(slots // pool_dev == my_index, code, 0)
        picked = jnp.where(session_group[None, :, None] == group_ids[:, None, None], code[None], 0)
        return jnp.sum(picked, axis=(1, 2))

    outgoing = pl.pallas_call(
        functools.partial(pack_kernel, seats=seats_group),
        in_specs=[vmem, vmem, vmem, hbm],
        out_specs=hbm,
        scratch_shapes=[
            pltpu.VMEM((group_count, kv_heads, block_len, pair_width), dtype),
            pltpu.SemaphoreType.DMA((group_count,)),
            pltpu.SemaphoreType.DMA((group_count,)),
        ],
        out_shape=jax.ShapeDtypeStruct((group_count, kv_heads, block_len, pair_width), dtype),
        compiler_params=pltpu.CompilerParams(vmem_limit_bytes=16 * 1024 * 1024),
        name="pack",
    )(old_slots, session_seat[None, :], cache_lens[None, :], kv_pool)
    received = lax.all_to_all(
        outgoing.reshape(owners, block_len, pair_width),
        ("grp", "tp"), split_axis=0, concat_axis=0, tiled=True,
    )

    seat_ids = group_index * seats_group + jnp.arange(seats_group, dtype=jnp.int32)
    mine = (session_seat[None, :] == seat_ids[:, None]).astype(jnp.int32)
    my_lens = jnp.sum(mine * cache_lens[None, :], axis=1)
    my_old = jnp.sum(mine[:, :, None] * (old_slots // pool_dev)[None], axis=1)
    my_new = jnp.sum(mine[:, :, None] * (new_slots // pool_dev)[None], axis=1)
    unpack_codes = codes(new_slots, cache_lens + turn)
    fresh = new_kv.reshape(seats_group, turn, pair_width)

    spill = turn // block_len + 1
    edge = (my_lens // block_len)[:, None]
    past = jnp.arange(max_blocks, dtype=jnp.int32)[None, :] - edge
    edge_row = owners + jnp.arange(seats_group, dtype=jnp.int32)[:, None] * spill + past
    pick = jnp.where(jnp.logical_and(past >= 0, past < spill), edge_row, my_old)
    edge_old = jnp.sum(jnp.where(past == 0, my_old, 0), axis=1)
    owner_ids = jnp.arange(owners, dtype=jnp.int32)
    from_owner = my_old[None] == owner_ids[:, None, None]
    pick_rows = jnp.sum(jnp.where(from_owner, pick[None], 0), axis=(1, 2))
    new_owner = jnp.sum(jnp.where(from_owner, my_new[None], 0), axis=(1, 2))
    leaving = pl.pallas_call(
        grow_kernel,
        grid_spec=pltpu.PrefetchScalarGridSpec(
            num_scalar_prefetch=4,
            grid=(1,),
            in_specs=[vmem, hbm],
            out_specs=hbm,
            scratch_shapes=[
                pltpu.VMEM((owners + seats_group * spill, block_len, pair_width), dtype),
                pltpu.VMEM((seats_group, block_len, pair_width), dtype),
                pltpu.SemaphoreType.DMA((8,)),
                pltpu.SemaphoreType.DMA,
                pltpu.SemaphoreType.DMA((seats_group,)),
            ],
        ),
        out_shape=jax.ShapeDtypeStruct((owners, block_len, pair_width), dtype),
        compiler_params=pltpu.CompilerParams(vmem_limit_bytes=20 * 1024 * 1024),
        name="grow",
    )(pick_rows, new_owner, edge_old, my_lens, fresh, received)
    arrived = lax.all_to_all(leaving, ("grp", "tp"), split_axis=0, concat_axis=0, tiled=True)

    attention = pl.pallas_call(
        attend_kernel,
        grid_spec=pltpu.PrefetchScalarGridSpec(
            num_scalar_prefetch=2,
            grid=(1,),
            in_specs=[vmem, vmem, hbm],
            out_specs=vmem,
            scratch_shapes=[
                pltpu.VMEM((seats_group, max_blocks * block_len, pair_width), dtype),
                pltpu.VMEM((2, turn, 2 * head_dim), jnp.float32),
                pltpu.VMEM((2, turn, head_dim), jnp.float32),
                pltpu.SemaphoreType.DMA((seats_group, max_blocks)),
            ],
        ),
        out_shape=jax.ShapeDtypeStruct(queries.shape, dtype),
        compiler_params=pltpu.CompilerParams(vmem_limit_bytes=40 * 1024 * 1024),
        cost_estimate=pl.CostEstimate(
            flops=4 * seats_group * heads * turn * max_blocks * block_len * head_dim,
            bytes_accessed=owners * block_len * pair_width * 2,
            transcendentals=seats_group * heads * turn * max_blocks * block_len,
        ),
        name="attend",
    )(my_old, my_lens, queries, fresh, received)

    new_pool = pl.pallas_call(
        unpack_kernel,
        grid_spec=pltpu.PrefetchScalarGridSpec(
            num_scalar_prefetch=1,
            grid=(1,),
            in_specs=[hbm],
            out_specs=hbm,
            scratch_shapes=[
                pltpu.VMEM((group_count, kv_heads, block_len, pair_width), dtype),
                pltpu.VMEM((kv_heads, block_len, pair_width), dtype),
                pltpu.SemaphoreType.DMA((group_count,)),
                pltpu.SemaphoreType.DMA((group_count,)),
            ],
        ),
        out_shape=jax.ShapeDtypeStruct(kv_pool.shape, dtype),
        compiler_params=pltpu.CompilerParams(vmem_limit_bytes=16 * 1024 * 1024),
        name="unpack",
    )(unpack_codes, arrived.reshape(group_count, kv_heads, block_len, pair_width))
    return attention, new_pool


def solution(mesh):
    in_specs = (
        P("grp", "tp", None, None),
        P("grp", "tp", None, None),
        P(("grp", "tp"), None, None, None),
        P(),
        P(),
        P(),
        P(),
    )
    out_specs = (P("grp", "tp", None, None), P(("grp", "tp"), None, None, None))
    return jax.shard_map(local, mesh=mesh, in_specs=in_specs, out_specs=out_specs, check_vma=False)
```

```python
import functools
import math

import jax
import jax.numpy as jnp
from jax import lax
from jax.experimental import pallas as pl
from jax.experimental.pallas import tpu as pltpu
from jax.sharding import PartitionSpec as P

MASKED = -1e30
CHUNK_BLOCKS = 8
VMEM_LIMIT = 60 * 1024 * 1024


def pack_kernel(slots_ref, seats_ref, lens_ref, pool_ref, out_ref, held, load_sems, store_sems, *, seats):
    count, tp_count, block_len = pool_ref.shape[:3]
    sessions, max_blocks = slots_ref.shape

    def load(i):
        return pltpu.make_async_copy(pool_ref.at[i], held.at[i], load_sems.at[i])

    def store(i, g):
        return pltpu.make_async_copy(held.at[i], out_ref.at[g], store_sems.at[i])

    for i in range(count):
        load(i).start()
    square = (sessions, sessions)
    diagonal = lax.broadcasted_iota(jnp.int32, square, 0) == lax.broadcasted_iota(jnp.int32, square, 1)

    def column(row):
        return jnp.sum(jnp.where(diagonal, row, 0), axis=1, keepdims=True)

    group = lax.div(column(seats_ref[...]), seats)
    start = lax.broadcasted_iota(jnp.int32, (sessions, max_blocks), 1) * block_len
    code = jnp.where(start < column(lens_ref[...]), group + 1, 0)
    my_index = lax.axis_index("grp") * tp_count + lax.axis_index("tp")
    slot = slots_ref[...] - my_index * count
    codes = [jnp.sum(jnp.where(slot == i, code, 0)) for i in range(count)]

    def forward(i):
        load(i).wait()
        pl.when(codes[i] > 0)(lambda: store(i, codes[i] - 1).start())

    for i in range(count):
        forward(i)
    for i in range(count):
        pl.when(codes[i] > 0)(lambda i=i: store(i, codes[i] - 1).wait())


def unpack_kernel(code_ref, arrived_ref, out_ref, held, zeros, load_sems, store_sems):
    count = out_ref.shape[0]

    def load(g):
        return pltpu.make_async_copy(arrived_ref.at[g], held.at[g], load_sems.at[g])

    def store(g, source):
        slot = lax.rem(code_ref[g], count)
        return pltpu.make_async_copy(source, out_ref.at[slot], store_sems.at[g])

    def forward(g):
        load(g).wait()
        store(g, held.at[g]).start()

    for g in range(count):
        pl.when(code_ref[g] >= count)(lambda g=g: load(g).start())
    zeros[...] = jnp.zeros_like(zeros)
    for g in range(count):
        pl.when(code_ref[g] < count)(lambda g=g: store(g, zeros).start())
    for g in range(count):
        pl.when(code_ref[g] >= count)(lambda g=g: forward(g))
    for g in range(count):
        store(g, zeros).wait()


def grow_kernel(
    pick_ref, dst_ref, edge_ref, lens_ref, fresh_ref, recv_ref, out_ref,
    held, edge_in, load_sems, store_sem, edge_sems,
):
    owners, block_len, width = recv_ref.shape
    seats, turn = fresh_ref.shape[:2]
    spill = turn // block_len + 1
    parts = load_sems.shape[0]
    share = owners // parts

    def load(c):
        rows = pl.ds(c * share, share)
        return pltpu.make_async_copy(recv_ref.at[rows], held.at[rows], load_sems.at[c])

    def edge_load(q):
        return pltpu.make_async_copy(recv_ref.at[edge_ref[q]], edge_in.at[q], edge_sems.at[q])

    for q in range(seats):
        edge_load(q).start()
    for c in range(parts):
        load(c).start()
    row = lax.broadcasted_iota(jnp.int32, (block_len, width), 0)
    for q in range(seats):
        rest = lax.rem(lens_ref[q], block_len)
        tail = jnp.zeros((block_len, width), jnp.float32)
        moved = jnp.concatenate([fresh_ref[q].astype(jnp.float32), tail], axis=0)
        moved = pltpu.roll(moved, rest, 0)
        edge_load(q).wait()
        first = jnp.where(row < rest, edge_in[q].astype(jnp.float32), moved[:block_len])
        held[owners + q * spill] = first.astype(held.dtype)
        for k in range(1, spill):
            later = moved[k * block_len : (k + 1) * block_len]
            held[owners + q * spill + k] = later.astype(held.dtype)
    for c in range(parts):
        load(c).wait()
        for o in range(c * share, (c + 1) * share):
            pltpu.make_async_copy(held.at[pick_ref[o]], out_ref.at[dst_ref[o]], store_sem).start()
    pltpu.make_async_copy(held.at[pl.ds(0, owners)], out_ref, store_sem).wait()


def attend_kernel(
    src_ref, lens_ref, queries_ref, fresh_ref, recv_ref, out_ref, cache, acc, high, sems
):
    seats, max_blocks = src_ref.shape
    block_len = recv_ref.shape[1]
    head_dim = queries_ref.shape[3]
    heads = queries_ref.shape[1]
    turn = queries_ref.shape[2]
    span = CHUNK_BLOCKS * block_len
    factor = head_dim ** (-0.5) * math.log2(math.e)
    pair = 2

    def row_copy(q, j):
        return pltpu.make_async_copy(
            recv_ref.at[src_ref[q, j]],
            cache.at[q, pl.ds(pl.multiple_of(j * block_len, block_len), block_len)],
            sems.at[q, j],
        )

    def blocks_of(q):
        return (lens_ref[q] + block_len - 1) // block_len

    def chunks_of(q):
        return (lens_ref[q] + span - 1) // span

    for q in range(seats):
        pl.loop(0, blocks_of(q))(lambda j, q=q: row_copy(q, j).start())

    def values_of(rows):
        ones = jnp.ones((rows.shape[0], head_dim), rows.dtype)
        return jnp.concatenate([rows[:, head_dim:], ones], axis=1)

    def score(query, rows):
        return (
            lax.dot_general(
                query, rows[:, :head_dim], (((1,), (1,)), ((), ())),
                preferred_element_type=jnp.float32,
            )
            * factor
        )

    def weigh(scores, top, rows):
        weights = jnp.exp2(scores - top).astype(jnp.bfloat16)
        return jnp.dot(weights, values_of(rows), preferred_element_type=jnp.float32)

    for q in range(seats):
        length = lens_ref[q]
        pl.loop(0, blocks_of(q))(lambda j, q=q: row_copy(q, j).wait())

        @pl.loop(blocks_of(q), chunks_of(q) * CHUNK_BLOCKS)
        def _(j, q=q):
            start = pl.multiple_of(j * block_len, block_len)
            cache[q, pl.ds(start, block_len)] = jnp.zeros((block_len, cache.shape[2]), cache.dtype)

        @pl.loop(0, heads // pair)
        def _(h, q=q, length=length):
            row = lax.broadcasted_iota(jnp.int32, (turn, turn), 0)
            column = lax.broadcasted_iota(jnp.int32, (turn, turn), 1)
            fresh = fresh_ref[q]
            for k in range(pair):
                scores = score(queries_ref[q, h * pair + k], fresh)
                scores = jnp.where(column <= row, scores, MASKED)
                top = jnp.max(scores, axis=1, keepdims=True)
                acc[k] = weigh(scores, top, fresh)
                high[k] = jnp.broadcast_to(top, high.shape[1:])

            def step(c, masked):
                start = pl.multiple_of(c * span, span)
                rows = cache[q, pl.ds(start, span)]
                for k in range(pair):
                    scores = score(queries_ref[q, h * pair + k], rows)
                    if masked:
                        position = start + lax.broadcasted_iota(jnp.int32, (1, span), 1)
                        scores = jnp.where(position < length, scores, MASKED)
                    old = high[k, :, :1]
                    top = jnp.maximum(old, jnp.max(scores, axis=1, keepdims=True))
                    acc[k] = acc[k] * jnp.exp2(old - top) + weigh(scores, top, rows)
                    high[k] = jnp.broadcast_to(top, high.shape[1:])

            full = length // span
            pl.loop(0, full)(lambda c: step(c, False))
            pl.when(length > full * span)(lambda: step(full, True))
            for k in range(pair):
                total = acc[k, :, head_dim : head_dim + 1]
                out_ref[q, h * pair + k] = (acc[k, :, :head_dim] / total).astype(out_ref.dtype)


def local(queries, new_kv, kv_pool, cache_lens, session_seat, old_slots, new_slots):
    group_count = lax.axis_size("grp")
    tp_count = lax.axis_size("tp")
    pool_dev, kv_heads, block_len, pair_width = kv_pool.shape
    seats_group, heads, turn, head_dim = queries.shape
    max_blocks = old_slots.shape[1]
    owners = group_count * tp_count
    assert pool_dev == group_count and kv_heads == tp_count
    group_index = lax.axis_index("grp")
    my_index = group_index * tp_count + lax.axis_index("tp")
    dtype = kv_pool.dtype
    hbm = pl.BlockSpec(memory_space=pltpu.HBM)
    vmem = pl.BlockSpec(memory_space=pltpu.VMEM)

    block_start = jnp.arange(max_blocks, dtype=jnp.int32)[None, :] * block_len
    session_group = session_seat // seats_group
    group_ids = jnp.arange(group_count, dtype=jnp.int32)

    def codes(slots, lengths):
        live = (block_start < lengths[:, None]).astype(jnp.int32)
        code = slots % pool_dev + pool_dev * live
        code = jnp.where(slots // pool_dev == my_index, code, 0)
        picked = jnp.where(session_group[None, :, None] == group_ids[:, None, None], code[None], 0)
        return jnp.sum(picked, axis=(1, 2))

    outgoing = pl.pallas_call(
        functools.partial(pack_kernel, seats=seats_group),
        in_specs=[vmem, vmem, vmem, hbm],
        out_specs=hbm,
        scratch_shapes=[
            pltpu.VMEM((group_count, kv_heads, block_len, pair_width), dtype),
            pltpu.SemaphoreType.DMA((group_count,)),
            pltpu.SemaphoreType.DMA((group_count,)),
        ],
        out_shape=jax.ShapeDtypeStruct((group_count, kv_heads, block_len, pair_width), dtype),
        compiler_params=pltpu.CompilerParams(vmem_limit_bytes=VMEM_LIMIT),
        name="pack",
    )(old_slots, session_seat[None, :], cache_lens[None, :], kv_pool)
    received = lax.all_to_all(
        outgoing.reshape(owners, block_len, pair_width),
        ("grp", "tp"), split_axis=0, concat_axis=0, tiled=True,
    )

    seat_ids = group_index * seats_group + jnp.arange(seats_group, dtype=jnp.int32)
    mine = (session_seat[None, :] == seat_ids[:, None]).astype(jnp.int32)
    my_lens = jnp.sum(mine * cache_lens[None, :], axis=1)
    my_old = jnp.sum(mine[:, :, None] * (old_slots // pool_dev)[None], axis=1)
    my_new = jnp.sum(mine[:, :, None] * (new_slots // pool_dev)[None], axis=1)
    unpack_codes = codes(new_slots, cache_lens + turn)
    fresh = new_kv.reshape(seats_group, turn, pair_width)

    spill = turn // block_len + 1
    edge = (my_lens // block_len)[:, None]
    past = jnp.arange(max_blocks, dtype=jnp.int32)[None, :] - edge
    edge_row = owners + jnp.arange(seats_group, dtype=jnp.int32)[:, None] * spill + past
    pick = jnp.where(jnp.logical_and(past >= 0, past < spill), edge_row, my_old)
    edge_old = jnp.sum(jnp.where(past == 0, my_old, 0), axis=1)
    owner_ids = jnp.arange(owners, dtype=jnp.int32)
    from_owner = my_old[None] == owner_ids[:, None, None]
    pick_rows = jnp.sum(jnp.where(from_owner, pick[None], 0), axis=(1, 2))
    new_owner = jnp.sum(jnp.where(from_owner, my_new[None], 0), axis=(1, 2))
    leaving = pl.pallas_call(
        grow_kernel,
        grid_spec=pltpu.PrefetchScalarGridSpec(
            num_scalar_prefetch=4,
            grid=(1,),
            in_specs=[vmem, hbm],
            out_specs=hbm,
            scratch_shapes=[
                pltpu.VMEM((owners + seats_group * spill, block_len, pair_width), dtype),
                pltpu.VMEM((seats_group, block_len, pair_width), dtype),
                pltpu.SemaphoreType.DMA((8,)),
                pltpu.SemaphoreType.DMA,
                pltpu.SemaphoreType.DMA((seats_group,)),
            ],
        ),
        out_shape=jax.ShapeDtypeStruct((owners, block_len, pair_width), dtype),
        compiler_params=pltpu.CompilerParams(vmem_limit_bytes=VMEM_LIMIT),
        name="grow",
    )(pick_rows, new_owner, edge_old, my_lens, fresh, received)
    arrived = lax.all_to_all(leaving, ("grp", "tp"), split_axis=0, concat_axis=0, tiled=True)

    attention = pl.pallas_call(
        attend_kernel,
        grid_spec=pltpu.PrefetchScalarGridSpec(
            num_scalar_prefetch=2,
            grid=(1,),
            in_specs=[vmem, vmem, hbm],
            out_specs=vmem,
            scratch_shapes=[
                pltpu.VMEM((seats_group, max_blocks * block_len, pair_width), dtype),
                pltpu.VMEM((2, turn, 2 * head_dim), jnp.float32),
                pltpu.VMEM((2, turn, head_dim), jnp.float32),
                pltpu.SemaphoreType.DMA((seats_group, max_blocks)),
            ],
        ),
        out_shape=jax.ShapeDtypeStruct(queries.shape, dtype),
        compiler_params=pltpu.CompilerParams(vmem_limit_bytes=VMEM_LIMIT),
        cost_estimate=pl.CostEstimate(
            flops=4 * seats_group * heads * turn * max_blocks * block_len * head_dim,
            bytes_accessed=owners * block_len * pair_width * 2,
            transcendentals=seats_group * heads * turn * max_blocks * block_len,
        ),
        name="attend",
    )(my_old, my_lens, queries, fresh, received)

    new_pool = pl.pallas_call(
        unpack_kernel,
        grid_spec=pltpu.PrefetchScalarGridSpec(
            num_scalar_prefetch=1,
            grid=(1,),
            in_specs=[hbm],
            out_specs=hbm,
            scratch_shapes=[
                pltpu.VMEM((group_count, kv_heads, block_len, pair_width), dtype),
                pltpu.VMEM((kv_heads, block_len, pair_width), dtype),
                pltpu.SemaphoreType.DMA((group_count,)),
                pltpu.SemaphoreType.DMA((group_count,)),
            ],
        ),
        out_shape=jax.ShapeDtypeStruct(kv_pool.shape, dtype),
        compiler_params=pltpu.CompilerParams(vmem_limit_bytes=VMEM_LIMIT),
        name="unpack",
    )(unpack_codes, arrived.reshape(group_count, kv_heads, block_len, pair_width))
    return attention, new_pool


def solution(mesh):
    in_specs = (
        P("grp", "tp", None, None),
        P("grp", "tp", None, None),
        P(("grp", "tp"), None, None, None),
        P(),
        P(),
        P(),
        P(),
    )
    out_specs = (P("grp", "tp", None, None), P(("grp", "tp"), None, None, None))
    return jax.shard_map(local, mesh=mesh, in_specs=in_specs, out_specs=out_specs, check_vma=False)
```

```python
import functools
import math

import jax
import jax.numpy as jnp
from jax import lax
from jax.experimental import pallas as pl
from jax.experimental.pallas import tpu as pltpu
from jax.sharding import PartitionSpec as P

MASKED = -1e30
CHUNK_BLOCKS = 8
PICK, TARGET, LENGTHS, EDGES, CODES, SOURCES = range(6)
TABLE_ROWS = 8
VMEM_LIMIT = 60 * 1024 * 1024
PACK_LIMIT = 40 * 1024 * 1024


def pack_kernel(
    packed_ref, pool_ref, out_ref, table_ref, sems, *, seats, turn
):
    count, tp_count, block_len = pool_ref.shape[:3]
    sessions, max_blocks = packed_ref.shape[0], packed_ref.shape[1] // 2
    owners = table_ref.shape[1]
    spill = turn // block_len + 1
    my_group = lax.axis_index("grp")
    first_slot = (my_group * tp_count + lax.axis_index("tp")) * count

    shape = (sessions, max_blocks)
    block = lax.broadcasted_iota(jnp.int32, shape, 1)
    slots = owners * count
    old = lax.rem(packed_ref[:, :max_blocks], slots)
    new = lax.div(packed_ref[:, :max_blocks], slots)
    length = lax.div(packed_ref[:, max_blocks:], sessions)
    seat = lax.rem(packed_ref[:, max_blocks:], sessions)
    group = lax.div(seat, seats)

    def codes_of(slots, lengths):
        code = jnp.where(block * block_len < lengths, group + 1, 0)
        return [jnp.sum(jnp.where(slots - first_slot == i, code, 0)) for i in range(count)]

    codes = codes_of(old, length)

    def copy(i):
        return pltpu.make_async_copy(pool_ref.at[i], out_ref.at[codes[i] - 1], sems.at[i])

    for i in range(count):
        pl.when(codes[i] > 0)(lambda i=i: copy(i).start())

    table_ref[...] = jnp.zeros_like(table_ref)
    lane = lax.broadcasted_iota(jnp.int32, (1, owners), 1)
    code_row = jnp.zeros((1, owners), jnp.int32)
    for i, code in enumerate(codes_of(new, length + turn)):
        code_row = jnp.where(lane == i, code, code_row)
    table_ref[CODES : CODES + 1, :] = code_row

    square = (max_blocks, max_blocks)
    diagonal = lax.broadcasted_iota(jnp.int32, square, 0) == lax.broadcasted_iota(jnp.int32, square, 1)
    owner = lax.broadcasted_iota(jnp.int32, (max_blocks, owners), 1)
    place = lax.broadcasted_iota(jnp.int32, (1, max_blocks), 1)
    pick_row = jnp.zeros((1, owners), jnp.int32)
    target_row = jnp.zeros((1, owners), jnp.int32)
    length_row = jnp.zeros((1, owners), jnp.int32)
    edge_row = jnp.zeros((1, owners), jnp.int32)
    for q in range(seats):
        mine = seat == my_group * seats + q

        def of_seat(values):
            return jnp.sum(jnp.where(mine, values, 0), axis=0, keepdims=True)

        def column(row):
            return jnp.sum(jnp.where(diagonal, row, 0), axis=1, keepdims=True)

        my_length = of_seat(length)
        source = of_seat(lax.div(old, count))
        past = place - lax.div(my_length, block_len)
        on_edge = jnp.logical_and(past >= 0, past < spill)
        pick = jnp.where(on_edge, owners + q * spill + past, source)
        from_owner = owner == column(source)
        pick_row += jnp.sum(jnp.where(from_owner, column(pick), 0), axis=0, keepdims=True)
        target = column(of_seat(lax.div(new, count)))
        target_row += jnp.sum(jnp.where(from_owner, target, 0), axis=0, keepdims=True)
        edge = jnp.sum(jnp.where(past == 0, source, 0), axis=1, keepdims=True)
        edge_row = jnp.where(lane == q, edge, edge_row)
        length_row = jnp.where(lane == q, my_length[:, :1], length_row)
        table_ref[SOURCES + q : SOURCES + q + 1, :max_blocks] = source
    table_ref[PICK : PICK + 1, :] = pick_row
    table_ref[TARGET : TARGET + 1, :] = target_row
    table_ref[LENGTHS : LENGTHS + 1, :] = length_row
    table_ref[EDGES : EDGES + 1, :] = edge_row
    for i in range(count):
        pl.when(codes[i] > 0)(lambda i=i: copy(i).wait())


def unpack_kernel(table_ref, arrived_ref, out_ref, held, zeros, load_sems, store_sems):
    count = out_ref.shape[0]

    def load(i):
        source = arrived_ref.at[table_ref[CODES, i] - 1]
        return pltpu.make_async_copy(source, held.at[i], load_sems.at[i])

    def store(i, source):
        return pltpu.make_async_copy(source, out_ref.at[i], store_sems.at[i])

    def forward(i):
        load(i).wait()
        store(i, held.at[i]).start()

    for i in range(count):
        pl.when(table_ref[CODES, i] > 0)(lambda i=i: load(i).start())
    zeros[...] = jnp.zeros_like(zeros)
    for i in range(count):
        pl.when(table_ref[CODES, i] == 0)(lambda i=i: store(i, zeros).start())
    for i in range(count):
        pl.when(table_ref[CODES, i] > 0)(lambda i=i: forward(i))
    for i in range(count):
        store(i, zeros).wait()


def grow_kernel(
    table_ref, fresh_ref, recv_ref, out_ref,
    held, edge_in, load_sems, store_sem, edge_sems,
):
    owners, block_len, width = recv_ref.shape
    seats, turn = fresh_ref.shape[:2]
    spill = turn // block_len + 1
    parts = load_sems.shape[0]
    share = owners // parts

    def load(c):
        rows = pl.ds(c * share, share)
        return pltpu.make_async_copy(recv_ref.at[rows], held.at[rows], load_sems.at[c])

    def edge_load(q):
        return pltpu.make_async_copy(recv_ref.at[table_ref[EDGES, q]], edge_in.at[q], edge_sems.at[q])

    for q in range(seats):
        edge_load(q).start()
    for c in range(parts):
        load(c).start()
    row = lax.broadcasted_iota(jnp.int32, (block_len, width), 0)
    for q in range(seats):
        rest = lax.rem(table_ref[LENGTHS, q], block_len)
        tail = jnp.zeros((block_len, width), jnp.float32)
        moved = jnp.concatenate([fresh_ref[q].astype(jnp.float32), tail], axis=0)
        moved = pltpu.roll(moved, rest, 0)
        edge_load(q).wait()
        first = jnp.where(row < rest, edge_in[q].astype(jnp.float32), moved[:block_len])
        held[owners + q * spill] = first.astype(held.dtype)
        for k in range(1, spill):
            later = moved[k * block_len : (k + 1) * block_len]
            held[owners + q * spill + k] = later.astype(held.dtype)
    for c in range(parts):
        load(c).wait()
        for o in range(c * share, (c + 1) * share):
            row_in, row_out = held.at[table_ref[PICK, o]], out_ref.at[table_ref[TARGET, o]]
            pltpu.make_async_copy(row_in, row_out, store_sem).start()
    pltpu.make_async_copy(held.at[pl.ds(0, owners)], out_ref, store_sem).wait()


def attend_kernel(
    table_ref, queries_ref, fresh_ref, recv_ref, out_ref, cache, acc, high, sems
):
    seats = queries_ref.shape[0]
    block_len = recv_ref.shape[1]
    head_dim = queries_ref.shape[3]
    heads = queries_ref.shape[1]
    turn = queries_ref.shape[2]
    span = CHUNK_BLOCKS * block_len
    factor = head_dim ** (-0.5) * math.log2(math.e)
    pair = 2

    def row_copy(q, j):
        return pltpu.make_async_copy(
            recv_ref.at[table_ref[SOURCES + q, j]],
            cache.at[q, pl.ds(pl.multiple_of(j * block_len, block_len), block_len)],
            sems.at[q, j],
        )

    def blocks_of(q):
        return (table_ref[LENGTHS, q] + block_len - 1) // block_len

    def chunks_of(q):
        return (table_ref[LENGTHS, q] + span - 1) // span

    for q in range(seats):
        pl.loop(0, blocks_of(q))(lambda j, q=q: row_copy(q, j).start())

    def values_of(rows):
        ones = jnp.ones((rows.shape[0], head_dim), rows.dtype)
        return jnp.concatenate([rows[:, head_dim:], ones], axis=1)

    def score(query, rows):
        return (
            lax.dot_general(
                query, rows[:, :head_dim], (((1,), (1,)), ((), ())),
                preferred_element_type=jnp.float32,
            )
            * factor
        )

    def weigh(scores, top, rows):
        weights = jnp.exp2(scores - top).astype(jnp.bfloat16)
        return jnp.dot(weights, values_of(rows), preferred_element_type=jnp.float32)

    for q in range(seats):
        length = table_ref[LENGTHS, q]
        pl.loop(0, blocks_of(q))(lambda j, q=q: row_copy(q, j).wait())

        @pl.loop(blocks_of(q), chunks_of(q) * CHUNK_BLOCKS)
        def _(j, q=q):
            start = pl.multiple_of(j * block_len, block_len)
            cache[q, pl.ds(start, block_len)] = jnp.zeros((block_len, cache.shape[2]), cache.dtype)

        @pl.loop(0, heads // pair)
        def _(h, q=q, length=length):
            row = lax.broadcasted_iota(jnp.int32, (turn, turn), 0)
            column = lax.broadcasted_iota(jnp.int32, (turn, turn), 1)
            fresh = fresh_ref[q]
            for k in range(pair):
                scores = score(queries_ref[q, h * pair + k], fresh)
                scores = jnp.where(column <= row, scores, MASKED)
                top = jnp.max(scores, axis=1, keepdims=True)
                acc[k] = weigh(scores, top, fresh)
                high[k] = jnp.broadcast_to(top, high.shape[1:])

            def step(c, masked):
                start = pl.multiple_of(c * span, span)
                rows = cache[q, pl.ds(start, span)]
                for k in range(pair):
                    scores = score(queries_ref[q, h * pair + k], rows)
                    if masked:
                        position = start + lax.broadcasted_iota(jnp.int32, (1, span), 1)
                        scores = jnp.where(position < length, scores, MASKED)
                    old = high[k, :, :1]
                    top = jnp.maximum(old, jnp.max(scores, axis=1, keepdims=True))
                    acc[k] = acc[k] * jnp.exp2(old - top) + weigh(scores, top, rows)
                    high[k] = jnp.broadcast_to(top, high.shape[1:])

            full = length // span
            pl.loop(0, full)(lambda c: step(c, False))
            pl.when(length > full * span)(lambda: step(full, True))
            for k in range(pair):
                total = acc[k, :, head_dim : head_dim + 1]
                out_ref[q, h * pair + k] = (acc[k, :, :head_dim] / total).astype(out_ref.dtype)


def local(queries, new_kv, kv_pool, cache_lens, session_seat, old_slots, new_slots):
    group_count = lax.axis_size("grp")
    tp_count = lax.axis_size("tp")
    pool_dev, kv_heads, block_len, pair_width = kv_pool.shape
    seats_group, heads, turn, head_dim = queries.shape
    max_blocks = old_slots.shape[1]
    owners = group_count * tp_count
    assert pool_dev == group_count and kv_heads == tp_count and max_blocks <= owners
    dtype = kv_pool.dtype
    anywhere = pl.BlockSpec(memory_space=pl.ANY)
    vmem = pl.BlockSpec(memory_space=pltpu.VMEM)
    smem = pl.BlockSpec(memory_space=pltpu.SMEM)
    rows = jax.ShapeDtypeStruct((owners, block_len, pair_width), dtype)
    blocks = jax.ShapeDtypeStruct((group_count, kv_heads, block_len, pair_width), dtype)
    fresh = new_kv.reshape(seats_group, turn, pair_width)
    spill = turn // block_len + 1

    session = cache_lens * session_seat.shape[0] + session_seat
    packed = jnp.concatenate(
        [new_slots * (owners * pool_dev) + old_slots, jnp.broadcast_to(session[:, None], old_slots.shape)],
        axis=1,
    )
    outgoing, table = pl.pallas_call(
        functools.partial(pack_kernel, seats=seats_group, turn=turn),
        in_specs=[vmem, anywhere],
        out_specs=[anywhere, vmem],
        scratch_shapes=[pltpu.SemaphoreType.DMA((group_count,))],
        out_shape=[blocks, jax.ShapeDtypeStruct((TABLE_ROWS, owners), jnp.int32)],
        compiler_params=pltpu.CompilerParams(vmem_limit_bytes=PACK_LIMIT),
        name="pack",
    )(packed, kv_pool)
    received = lax.all_to_all(
        outgoing.reshape(rows.shape), ("grp", "tp"), split_axis=0, concat_axis=0, tiled=True
    )

    leaving = pl.pallas_call(
        grow_kernel,
        in_specs=[smem, vmem, anywhere],
        out_specs=anywhere,
        scratch_shapes=[
            pltpu.VMEM((owners + seats_group * spill, block_len, pair_width), dtype),
            pltpu.VMEM((seats_group, block_len, pair_width), dtype),
            pltpu.SemaphoreType.DMA((8,)),
            pltpu.SemaphoreType.DMA,
            pltpu.SemaphoreType.DMA((seats_group,)),
        ],
        out_shape=rows,
        compiler_params=pltpu.CompilerParams(vmem_limit_bytes=VMEM_LIMIT),
        name="grow",
    )(table, fresh, received)
    arrived = lax.all_to_all(leaving, ("grp", "tp"), split_axis=0, concat_axis=0, tiled=True)

    attention = pl.pallas_call(
        attend_kernel,
        in_specs=[smem, vmem, vmem, anywhere],
        out_specs=vmem,
        scratch_shapes=[
            pltpu.VMEM((seats_group, max_blocks * block_len, pair_width), dtype),
            pltpu.VMEM((2, turn, 2 * head_dim), jnp.float32),
            pltpu.VMEM((2, turn, head_dim), jnp.float32),
            pltpu.SemaphoreType.DMA((seats_group, max_blocks)),
        ],
        out_shape=jax.ShapeDtypeStruct(queries.shape, dtype),
        compiler_params=pltpu.CompilerParams(vmem_limit_bytes=VMEM_LIMIT),
        cost_estimate=pl.CostEstimate(
            flops=4 * seats_group * heads * turn * max_blocks * block_len * head_dim,
            bytes_accessed=owners * block_len * pair_width * 2,
            transcendentals=seats_group * heads * turn * max_blocks * block_len,
        ),
        name="attend",
    )(table, queries, fresh, received)

    new_pool = pl.pallas_call(
        unpack_kernel,
        in_specs=[smem, anywhere],
        out_specs=anywhere,
        scratch_shapes=[
            pltpu.VMEM(blocks.shape, dtype),
            pltpu.VMEM(blocks.shape[1:], dtype),
            pltpu.SemaphoreType.DMA((group_count,)),
            pltpu.SemaphoreType.DMA((group_count,)),
        ],
        out_shape=blocks,
        compiler_params=pltpu.CompilerParams(vmem_limit_bytes=VMEM_LIMIT),
        name="unpack",
    )(table, arrived.reshape(blocks.shape))
    return attention, new_pool


def solution(mesh):
    in_specs = (
        P("grp", "tp", None, None),
        P("grp", "tp", None, None),
        P(("grp", "tp"), None, None, None),
        P(),
        P(),
        P(),
        P(),
    )
    out_specs = (P("grp", "tp", None, None), P(("grp", "tp"), None, None, None))
    return jax.shard_map(local, mesh=mesh, in_specs=in_specs, out_specs=out_specs, check_vma=False)
```

```python
import functools
import math

import jax
import jax.numpy as jnp
from jax import lax
from jax.experimental import pallas as pl
from jax.experimental.pallas import tpu as pltpu
from jax.sharding import PartitionSpec as P

MASKED = -1e30
CHUNK_BLOCKS = 8
PICK, TARGET, LENGTHS, EDGES, CODES, BLOCKS = range(6)
TABLE_ROWS = 8
VMEM_LIMIT = 60 * 1024 * 1024
PACK_LIMIT = 24 * 1024 * 1024
GROW_LIMIT = 24 * 1024 * 1024
ATTEND_LIMIT = 60 * 1024 * 1024


def pack_kernel(
    seat_ref, lens_ref, old_ref, new_ref, pool_ref, out_ref, table_ref, sems, *, seats, turn
):
    count, tp_count, block_len = pool_ref.shape[:3]
    sessions, max_blocks = old_ref.shape
    owners = table_ref.shape[1]
    spill = turn // block_len + 1
    my_group = lax.axis_index("grp")
    first_slot = (my_group * tp_count + lax.axis_index("tp")) * count

    shape = (sessions, max_blocks)
    session = lax.broadcasted_iota(jnp.int32, shape, 0)
    block = lax.broadcasted_iota(jnp.int32, shape, 1)
    seat = jnp.zeros(shape, jnp.int32)
    length = jnp.zeros(shape, jnp.int32)
    for s in range(sessions):
        seat = jnp.where(session == s, seat_ref[s], seat)
        length = jnp.where(session == s, lens_ref[s], length)
    group = lax.div(seat, seats)

    def codes_of(slots, lengths):
        code = jnp.where(block * block_len < lengths, group + 1, 0)
        return [jnp.sum(jnp.where(slots - first_slot == i, code, 0)) for i in range(count)]

    old = old_ref[...]
    new = new_ref[...]
    codes = codes_of(old, length)

    def copy(i):
        return pltpu.make_async_copy(pool_ref.at[i], out_ref.at[codes[i] - 1], sems.at[i])

    for i in range(count):
        pl.when(codes[i] > 0)(lambda i=i: copy(i).start())

    table_ref[...] = jnp.zeros_like(table_ref)
    lane = lax.broadcasted_iota(jnp.int32, (1, owners), 1)
    code_row = jnp.zeros((1, owners), jnp.int32)
    for i, code in enumerate(codes_of(new, length + turn)):
        code_row = jnp.where(lane == i, code, code_row)
    table_ref[CODES : CODES + 1, :] = code_row

    square = (max_blocks, max_blocks)
    diagonal = lax.broadcasted_iota(jnp.int32, square, 0) == lax.broadcasted_iota(jnp.int32, square, 1)
    owner = lax.broadcasted_iota(jnp.int32, (max_blocks, owners), 1)
    place = lax.broadcasted_iota(jnp.int32, (1, max_blocks), 1)
    pick_row = jnp.zeros((1, owners), jnp.int32)
    target_row = jnp.zeros((1, owners), jnp.int32)
    length_row = jnp.zeros((1, owners), jnp.int32)
    edge_row = jnp.zeros((1, owners), jnp.int32)
    for q in range(seats):
        mine = seat == my_group * seats + q

        def of_seat(values):
            return jnp.sum(jnp.where(mine, values, 0), axis=0, keepdims=True)

        def column(row):
            return jnp.sum(jnp.where(diagonal, row, 0), axis=1, keepdims=True)

        my_length = of_seat(length)
        source = of_seat(lax.div(old, count))
        past = place - lax.div(my_length, block_len)
        on_edge = jnp.logical_and(past >= 0, past < spill)
        pick = jnp.where(on_edge, owners + q * spill + past, source)
        from_owner = owner == column(source)
        pick_row += jnp.sum(jnp.where(from_owner, column(pick), 0), axis=0, keepdims=True)
        target = of_seat(lax.div(new, count))
        target_row += jnp.sum(jnp.where(from_owner, column(target), 0), axis=0, keepdims=True)
        edge = jnp.sum(jnp.where(past == 0, source, 0), axis=1, keepdims=True)
        edge_row = jnp.where(lane == q, edge, edge_row)
        length_row = jnp.where(lane == q, my_length[:, :1], length_row)
        table_ref[BLOCKS + q : BLOCKS + q + 1, :max_blocks] = target
    table_ref[PICK : PICK + 1, :] = pick_row
    table_ref[TARGET : TARGET + 1, :] = target_row
    table_ref[LENGTHS : LENGTHS + 1, :] = length_row
    table_ref[EDGES : EDGES + 1, :] = edge_row
    for i in range(count):
        pl.when(codes[i] > 0)(lambda i=i: copy(i).wait())


def unpack_kernel(table_ref, arrived_ref, out_ref, held, zeros, load_sems, store_sems):
    count = out_ref.shape[0]

    def load(i):
        source = arrived_ref.at[table_ref[CODES, i] - 1]
        return pltpu.make_async_copy(source, held.at[i], load_sems.at[i])

    def store(i, source):
        return pltpu.make_async_copy(source, out_ref.at[i], store_sems.at[i])

    def forward(i):
        load(i).wait()
        store(i, held.at[i]).start()

    for i in range(count):
        pl.when(table_ref[CODES, i] > 0)(lambda i=i: load(i).start())
    zeros[...] = jnp.zeros_like(zeros)
    for i in range(count):
        pl.when(table_ref[CODES, i] == 0)(lambda i=i: store(i, zeros).start())
    for i in range(count):
        pl.when(table_ref[CODES, i] > 0)(lambda i=i: forward(i))
    for i in range(count):
        store(i, zeros).wait()


def grow_kernel(
    table_ref, fresh_ref, recv_ref, out_ref, grown, edge_in, store_sem, edge_sems
):
    owners, block_len, width = recv_ref.shape
    seats, turn = fresh_ref.shape[:2]
    spill = turn // block_len + 1

    def edge_load(q):
        row = recv_ref.at[table_ref[EDGES, q]]
        return pltpu.make_async_copy(row, edge_in.at[q], edge_sems.at[q])

    def send(o, source):
        pltpu.make_async_copy(source, out_ref.at[table_ref[TARGET, o]], store_sem).start()

    for q in range(seats):
        edge_load(q).start()
    for o in range(owners):
        pl.when(table_ref[PICK, o] < owners)(lambda o=o: send(o, recv_ref.at[o]))
    row = lax.broadcasted_iota(jnp.int32, (block_len, width), 0)
    for q in range(seats):
        rest = lax.rem(table_ref[LENGTHS, q], block_len)
        tail = jnp.zeros((block_len, width), jnp.float32)
        moved = jnp.concatenate([fresh_ref[q].astype(jnp.float32), tail], axis=0)
        moved = pltpu.roll(moved, rest, 0)
        edge_load(q).wait()
        first = jnp.where(row < rest, edge_in[q].astype(jnp.float32), moved[:block_len])
        grown[q * spill] = first.astype(grown.dtype)
        for k in range(1, spill):
            later = moved[k * block_len : (k + 1) * block_len]
            grown[q * spill + k] = later.astype(grown.dtype)

    @pl.loop(0, owners)
    def _(o):
        pick = table_ref[PICK, o]
        pl.when(pick >= owners)(lambda: send(o, grown.at[pick - owners]))

    pltpu.make_async_copy(recv_ref, out_ref, store_sem).wait()


def attend_kernel(
    table_ref, queries_ref, fresh_ref, grown_ref, out_ref, cache, acc, high, sems
):
    seats = queries_ref.shape[0]
    block_len = grown_ref.shape[1]
    head_dim = queries_ref.shape[3]
    heads = queries_ref.shape[1]
    turn = queries_ref.shape[2]
    span = CHUNK_BLOCKS * block_len
    factor = head_dim ** (-0.5) * math.log2(math.e)
    pair = 2

    def row_copy(q, j):
        return pltpu.make_async_copy(
            grown_ref.at[table_ref[BLOCKS + q, j]],
            cache.at[q, pl.ds(pl.multiple_of(j * block_len, block_len), block_len)],
            sems.at[q, j],
        )

    def blocks_of(q):
        return (table_ref[LENGTHS, q] + block_len - 1) // block_len

    def chunks_of(q):
        return (table_ref[LENGTHS, q] + span - 1) // span

    for q in range(seats):
        pl.loop(0, blocks_of(q))(lambda j, q=q: row_copy(q, j).start())

    def values_of(rows):
        ones = jnp.ones((rows.shape[0], head_dim), rows.dtype)
        return jnp.concatenate([rows[:, head_dim:], ones], axis=1)

    def score(query, rows):
        return (
            lax.dot_general(
                query, rows[:, :head_dim], (((1,), (1,)), ((), ())),
                preferred_element_type=jnp.float32,
            )
            * factor
        )

    def weigh(scores, top, rows):
        weights = jnp.exp2(scores - top).astype(jnp.bfloat16)
        return jnp.dot(weights, values_of(rows), preferred_element_type=jnp.float32)

    for q in range(seats):
        length = table_ref[LENGTHS, q]
        pl.loop(0, blocks_of(q))(lambda j, q=q: row_copy(q, j).wait())

        @pl.loop(blocks_of(q), chunks_of(q) * CHUNK_BLOCKS)
        def _(j, q=q):
            start = pl.multiple_of(j * block_len, block_len)
            cache[q, pl.ds(start, block_len)] = jnp.zeros((block_len, cache.shape[2]), cache.dtype)

        @pl.loop(0, heads // pair)
        def _(h, q=q, length=length):
            row = lax.broadcasted_iota(jnp.int32, (turn, turn), 0)
            column = lax.broadcasted_iota(jnp.int32, (turn, turn), 1)
            fresh = fresh_ref[q]
            for k in range(pair):
                scores = score(queries_ref[q, h * pair + k], fresh)
                scores = jnp.where(column <= row, scores, MASKED)
                top = jnp.max(scores, axis=1, keepdims=True)
                acc[k] = weigh(scores, top, fresh)
                high[k] = jnp.broadcast_to(top, high.shape[1:])

            def step(c, masked):
                start = pl.multiple_of(c * span, span)
                rows = cache[q, pl.ds(start, span)]
                for k in range(pair):
                    scores = score(queries_ref[q, h * pair + k], rows)
                    if masked:
                        position = start + lax.broadcasted_iota(jnp.int32, (1, span), 1)
                        scores = jnp.where(position < length, scores, MASKED)
                    old = high[k, :, :1]
                    top = jnp.maximum(old, jnp.max(scores, axis=1, keepdims=True))
                    acc[k] = acc[k] * jnp.exp2(old - top) + weigh(scores, top, rows)
                    high[k] = jnp.broadcast_to(top, high.shape[1:])

            full = length // span
            pl.loop(0, full)(lambda c: step(c, False))
            pl.when(length > full * span)(lambda: step(full, True))
            for k in range(pair):
                total = acc[k, :, head_dim : head_dim + 1]
                out_ref[q, h * pair + k] = (acc[k, :, :head_dim] / total).astype(out_ref.dtype)


def local(queries, new_kv, kv_pool, cache_lens, session_seat, old_slots, new_slots):
    group_count = lax.axis_size("grp")
    tp_count = lax.axis_size("tp")
    pool_dev, kv_heads, block_len, pair_width = kv_pool.shape
    seats_group, heads, turn, head_dim = queries.shape
    max_blocks = old_slots.shape[1]
    owners = group_count * tp_count
    assert pool_dev == group_count and kv_heads == tp_count and max_blocks <= owners
    dtype = kv_pool.dtype
    in_hbm = functools.partial(pltpu.with_memory_space_constraint, memory_space=pltpu.HBM)
    anywhere = pl.BlockSpec(memory_space=pl.ANY)
    vmem = pl.BlockSpec(memory_space=pltpu.VMEM)
    smem = pl.BlockSpec(memory_space=pltpu.SMEM)
    rows = jax.ShapeDtypeStruct((owners, block_len, pair_width), dtype)
    blocks = jax.ShapeDtypeStruct((group_count, kv_heads, block_len, pair_width), dtype)
    fresh = new_kv.reshape(seats_group, turn, pair_width)
    spill = turn // block_len + 1

    outgoing, table = pl.pallas_call(
        functools.partial(pack_kernel, seats=seats_group, turn=turn),
        in_specs=[smem, smem, vmem, vmem, anywhere],
        out_specs=[anywhere, vmem],
        scratch_shapes=[pltpu.SemaphoreType.DMA((group_count,))],
        out_shape=[pltpu.VMEM(blocks.shape, dtype), pltpu.HBM((TABLE_ROWS, owners), jnp.int32)],
        compiler_params=pltpu.CompilerParams(vmem_limit_bytes=PACK_LIMIT),
        name="pack",
    )(*map(in_hbm, (session_seat, cache_lens, old_slots, new_slots, kv_pool)))
    received = lax.all_to_all(
        outgoing.reshape(rows.shape), ("grp", "tp"), split_axis=0, concat_axis=0, tiled=True
    )

    leaving = pl.pallas_call(
        grow_kernel,
        in_specs=[smem, vmem, anywhere],
        out_specs=anywhere,
        scratch_shapes=[
            pltpu.VMEM((seats_group * spill, block_len, pair_width), dtype),
            pltpu.VMEM((seats_group, block_len, pair_width), dtype),
            pltpu.SemaphoreType.DMA,
            pltpu.SemaphoreType.DMA((seats_group,)),
        ],
        out_shape=pltpu.HBM(rows.shape, dtype),
        compiler_params=pltpu.CompilerParams(vmem_limit_bytes=GROW_LIMIT),
        name="grow",
    )(table, fresh, pltpu.with_memory_space_constraint(received, pltpu.VMEM))
    arrived = lax.all_to_all(leaving, ("grp", "tp"), split_axis=0, concat_axis=0, tiled=True)

    attention = pl.pallas_call(
        attend_kernel,
        in_specs=[smem, vmem, vmem, anywhere],
        out_specs=vmem,
        scratch_shapes=[
            pltpu.VMEM((seats_group, max_blocks * block_len, pair_width), dtype),
            pltpu.VMEM((2, turn, 2 * head_dim), jnp.float32),
            pltpu.VMEM((2, turn, head_dim), jnp.float32),
            pltpu.SemaphoreType.DMA((seats_group, max_blocks)),
        ],
        out_shape=jax.ShapeDtypeStruct(queries.shape, dtype),
        compiler_params=pltpu.CompilerParams(vmem_limit_bytes=ATTEND_LIMIT),
        cost_estimate=pl.CostEstimate(
            flops=4 * seats_group * heads * turn * max_blocks * block_len * head_dim,
            bytes_accessed=owners * block_len * pair_width * 2,
            transcendentals=seats_group * heads * turn * max_blocks * block_len,
        ),
        name="attend",
    )(table, in_hbm(queries), fresh, in_hbm(leaving))

    new_pool = pl.pallas_call(
        unpack_kernel,
        in_specs=[smem, anywhere],
        out_specs=anywhere,
        scratch_shapes=[
            pltpu.VMEM(blocks.shape, dtype),
            pltpu.VMEM(blocks.shape[1:], dtype),
            pltpu.SemaphoreType.DMA((group_count,)),
            pltpu.SemaphoreType.DMA((group_count,)),
        ],
        out_shape=blocks,
        compiler_params=pltpu.CompilerParams(vmem_limit_bytes=VMEM_LIMIT),
        name="unpack",
    )(table, arrived.reshape(blocks.shape))
    return attention, new_pool


def solution(mesh):
    in_specs = (
        P("grp", "tp", None, None),
        P("grp", "tp", None, None),
        P(("grp", "tp"), None, None, None),
        P(),
        P(),
        P(),
        P(),
    )
    out_specs = (P("grp", "tp", None, None), P(("grp", "tp"), None, None, None))
    return jax.shard_map(local, mesh=mesh, in_specs=in_specs, out_specs=out_specs, check_vma=False)
```

```python
import functools
import math

import jax
import jax.numpy as jnp
from jax import lax
from jax.experimental import pallas as pl
from jax.experimental.pallas import tpu as pltpu
from jax.sharding import PartitionSpec as P

MASKED = -1e30
CHUNK_BLOCKS = 8
PICK, TARGET, LENGTHS, EDGES, CODES, BLOCKS = range(6)
TABLE_ROWS = 8
VMEM_LIMIT = 60 * 1024 * 1024
PACK_LIMIT = 24 * 1024 * 1024
GROW_LIMIT = 24 * 1024 * 1024
ATTEND_LIMIT = 60 * 1024 * 1024


def pack_kernel(
    seat_ref, lens_ref, old_ref, new_ref, pool_ref, out_ref, table_ref, sems, *, seats, turn
):
    count, tp_count, block_len = pool_ref.shape[:3]
    groups = out_ref.shape[1]
    sessions, max_blocks = old_ref.shape
    owners = table_ref.shape[1]
    spill = turn // block_len + 1
    my_group = lax.axis_index("grp")
    first_slot = (my_group * tp_count + lax.axis_index("tp")) * count

    shape = (sessions, max_blocks)
    session = lax.broadcasted_iota(jnp.int32, shape, 0)
    block = lax.broadcasted_iota(jnp.int32, shape, 1)
    seat = jnp.zeros(shape, jnp.int32)
    length = jnp.zeros(shape, jnp.int32)
    for s in range(sessions):
        seat = jnp.where(session == s, seat_ref[s], seat)
        length = jnp.where(session == s, lens_ref[s], length)
    group = lax.div(seat, seats)

    def codes_of(slots, lengths):
        code = jnp.where(block * block_len < lengths, group + 1, 0)
        return [jnp.sum(jnp.where(slots - first_slot == i, code, 0)) for i in range(count)]

    old = old_ref[...]
    new = new_ref[...]

    def rank_of(slots):
        device = lax.div(slots, count)
        return lax.rem(device, tp_count) * groups + lax.div(device, tp_count)

    codes = codes_of(old, length)

    def copy(i):
        return pltpu.make_async_copy(pool_ref.at[i], out_ref.at[:, codes[i] - 1], sems.at[i])

    for i in range(count):
        pl.when(codes[i] > 0)(lambda i=i: copy(i).start())

    table_ref[...] = jnp.zeros_like(table_ref)
    lane = lax.broadcasted_iota(jnp.int32, (1, owners), 1)
    code_row = jnp.zeros((1, owners), jnp.int32)
    for i, code in enumerate(codes_of(new, length + turn)):
        code_row = jnp.where(lane == i, code, code_row)
    table_ref[CODES : CODES + 1, :] = code_row

    square = (max_blocks, max_blocks)
    diagonal = lax.broadcasted_iota(jnp.int32, square, 0) == lax.broadcasted_iota(jnp.int32, square, 1)
    owner = lax.broadcasted_iota(jnp.int32, (max_blocks, owners), 1)
    place = lax.broadcasted_iota(jnp.int32, (1, max_blocks), 1)
    pick_row = jnp.zeros((1, owners), jnp.int32)
    target_row = jnp.zeros((1, owners), jnp.int32)
    length_row = jnp.zeros((1, owners), jnp.int32)
    edge_row = jnp.zeros((1, owners), jnp.int32)
    for q in range(seats):
        mine = seat == my_group * seats + q

        def of_seat(values):
            return jnp.sum(jnp.where(mine, values, 0), axis=0, keepdims=True)

        def column(row):
            return jnp.sum(jnp.where(diagonal, row, 0), axis=1, keepdims=True)

        my_length = of_seat(length)
        source = of_seat(rank_of(old))
        past = place - lax.div(my_length, block_len)
        on_edge = jnp.logical_and(past >= 0, past < spill)
        pick = jnp.where(on_edge, owners + q * spill + past, source)
        from_owner = owner == column(source)
        pick_row += jnp.sum(jnp.where(from_owner, column(pick), 0), axis=0, keepdims=True)
        target = of_seat(rank_of(new))
        target_row += jnp.sum(jnp.where(from_owner, column(target), 0), axis=0, keepdims=True)
        edge = jnp.sum(jnp.where(past == 0, source, 0), axis=1, keepdims=True)
        edge_row = jnp.where(lane == q, edge, edge_row)
        length_row = jnp.where(lane == q, my_length[:, :1], length_row)
        table_ref[BLOCKS + q : BLOCKS + q + 1, :max_blocks] = target
    table_ref[PICK : PICK + 1, :] = pick_row
    table_ref[TARGET : TARGET + 1, :] = target_row
    table_ref[LENGTHS : LENGTHS + 1, :] = length_row
    table_ref[EDGES : EDGES + 1, :] = edge_row
    for i in range(count):
        pl.when(codes[i] > 0)(lambda i=i: copy(i).wait())


def unpack_kernel(table_ref, arrived_ref, out_ref, held, zeros, load_sems, store_sems):
    count = out_ref.shape[0]

    def load(i):
        source = arrived_ref.at[:, table_ref[CODES, i] - 1]
        return pltpu.make_async_copy(source, held.at[i], load_sems.at[i])

    def store(i, source):
        return pltpu.make_async_copy(source, out_ref.at[i], store_sems.at[i])

    def forward(i):
        load(i).wait()
        store(i, held.at[i]).start()

    for i in range(count):
        pl.when(table_ref[CODES, i] > 0)(lambda i=i: load(i).start())
    zeros[...] = jnp.zeros_like(zeros)
    for i in range(count):
        pl.when(table_ref[CODES, i] == 0)(lambda i=i: store(i, zeros).start())
    for i in range(count):
        pl.when(table_ref[CODES, i] > 0)(lambda i=i: forward(i))
    for i in range(count):
        store(i, zeros).wait()


def grow_kernel(
    table_ref, fresh_ref, recv_ref, out_ref, grown, edge_in, store_sem, edge_sems
):
    owners, block_len, width = recv_ref.shape
    seats, turn = fresh_ref.shape[:2]
    spill = turn // block_len + 1

    def edge_load(q):
        row = recv_ref.at[table_ref[EDGES, q]]
        return pltpu.make_async_copy(row, edge_in.at[q], edge_sems.at[q])

    def send(o, source):
        pltpu.make_async_copy(source, out_ref.at[table_ref[TARGET, o]], store_sem).start()

    for q in range(seats):
        edge_load(q).start()
    for o in range(owners):
        pl.when(table_ref[PICK, o] < owners)(lambda o=o: send(o, recv_ref.at[o]))
    row = lax.broadcasted_iota(jnp.int32, (block_len, width), 0)
    for q in range(seats):
        rest = lax.rem(table_ref[LENGTHS, q], block_len)
        tail = jnp.zeros((block_len, width), jnp.float32)
        moved = jnp.concatenate([fresh_ref[q].astype(jnp.float32), tail], axis=0)
        moved = pltpu.roll(moved, rest, 0)
        edge_load(q).wait()
        first = jnp.where(row < rest, edge_in[q].astype(jnp.float32), moved[:block_len])
        grown[q * spill] = first.astype(grown.dtype)
        for k in range(1, spill):
            later = moved[k * block_len : (k + 1) * block_len]
            grown[q * spill + k] = later.astype(grown.dtype)

    @pl.loop(0, owners)
    def _(o):
        pick = table_ref[PICK, o]
        pl.when(pick >= owners)(lambda: send(o, grown.at[pick - owners]))

    pltpu.make_async_copy(recv_ref, out_ref, store_sem).wait()


def attend_kernel(
    table_ref, queries_ref, fresh_ref, grown_ref, out_ref, cache, acc, high, sems
):
    seats = queries_ref.shape[0]
    block_len = grown_ref.shape[1]
    head_dim = queries_ref.shape[3]
    heads = queries_ref.shape[1]
    turn = queries_ref.shape[2]
    span = CHUNK_BLOCKS * block_len
    factor = head_dim ** (-0.5) * math.log2(math.e)
    pair = 2

    def row_copy(q, j):
        return pltpu.make_async_copy(
            grown_ref.at[table_ref[BLOCKS + q, j]],
            cache.at[q, pl.ds(pl.multiple_of(j * block_len, block_len), block_len)],
            sems.at[q, j],
        )

    def blocks_of(q):
        return (table_ref[LENGTHS, q] + block_len - 1) // block_len

    def chunks_of(q):
        return (table_ref[LENGTHS, q] + span - 1) // span

    for q in range(seats):
        pl.loop(0, blocks_of(q))(lambda j, q=q: row_copy(q, j).start())

    def values_of(rows):
        ones = jnp.ones((rows.shape[0], head_dim), rows.dtype)
        return jnp.concatenate([rows[:, head_dim:], ones], axis=1)

    def score(query, rows):
        return (
            lax.dot_general(
                query, rows[:, :head_dim], (((1,), (1,)), ((), ())),
                preferred_element_type=jnp.float32,
            )
            * factor
        )

    def weigh(scores, top, rows):
        weights = jnp.exp2(scores - top).astype(jnp.bfloat16)
        return jnp.dot(weights, values_of(rows), preferred_element_type=jnp.float32)

    for q in range(seats):
        length = table_ref[LENGTHS, q]
        pl.loop(0, blocks_of(q))(lambda j, q=q: row_copy(q, j).wait())

        @pl.loop(blocks_of(q), chunks_of(q) * CHUNK_BLOCKS)
        def _(j, q=q):
            start = pl.multiple_of(j * block_len, block_len)
            cache[q, pl.ds(start, block_len)] = jnp.zeros((block_len, cache.shape[2]), cache.dtype)

        @pl.loop(0, heads // pair)
        def _(h, q=q, length=length):
            row = lax.broadcasted_iota(jnp.int32, (turn, turn), 0)
            column = lax.broadcasted_iota(jnp.int32, (turn, turn), 1)
            fresh = fresh_ref[q]
            for k in range(pair):
                scores = score(queries_ref[q, h * pair + k], fresh)
                scores = jnp.where(column <= row, scores, MASKED)
                top = jnp.max(scores, axis=1, keepdims=True)
                acc[k] = weigh(scores, top, fresh)
                high[k] = jnp.broadcast_to(top, high.shape[1:])

            def step(c, masked):
                start = pl.multiple_of(c * span, span)
                rows = cache[q, pl.ds(start, span)]
                for k in range(pair):
                    scores = score(queries_ref[q, h * pair + k], rows)
                    if masked:
                        position = start + lax.broadcasted_iota(jnp.int32, (1, span), 1)
                        scores = jnp.where(position < length, scores, MASKED)
                    old = high[k, :, :1]
                    top = jnp.maximum(old, jnp.max(scores, axis=1, keepdims=True))
                    acc[k] = acc[k] * jnp.exp2(old - top) + weigh(scores, top, rows)
                    high[k] = jnp.broadcast_to(top, high.shape[1:])

            full = length // span
            pl.loop(0, full)(lambda c: step(c, False))
            pl.when(length > full * span)(lambda: step(full, True))
            for k in range(pair):
                total = acc[k, :, head_dim : head_dim + 1]
                out_ref[q, h * pair + k] = (acc[k, :, :head_dim] / total).astype(out_ref.dtype)


def local(queries, new_kv, kv_pool, cache_lens, session_seat, old_slots, new_slots):
    group_count = lax.axis_size("grp")
    tp_count = lax.axis_size("tp")
    pool_dev, kv_heads, block_len, pair_width = kv_pool.shape
    seats_group, heads, turn, head_dim = queries.shape
    max_blocks = old_slots.shape[1]
    owners = group_count * tp_count
    assert pool_dev == group_count and kv_heads == tp_count and max_blocks <= owners
    dtype = kv_pool.dtype
    in_hbm = functools.partial(pltpu.with_memory_space_constraint, memory_space=pltpu.HBM)
    anywhere = pl.BlockSpec(memory_space=pl.ANY)
    vmem = pl.BlockSpec(memory_space=pltpu.VMEM)
    smem = pl.BlockSpec(memory_space=pltpu.SMEM)
    rows = jax.ShapeDtypeStruct((owners, block_len, pair_width), dtype)
    blocks = jax.ShapeDtypeStruct((group_count, kv_heads, block_len, pair_width), dtype)
    by_head = jax.ShapeDtypeStruct((kv_heads, group_count, block_len, pair_width), dtype)
    fresh = new_kv.reshape(seats_group, turn, pair_width)
    spill = turn // block_len + 1

    outgoing, table = pl.pallas_call(
        functools.partial(pack_kernel, seats=seats_group, turn=turn),
        in_specs=[smem, smem, vmem, vmem, anywhere],
        out_specs=[anywhere, vmem],
        scratch_shapes=[pltpu.SemaphoreType.DMA((group_count,))],
        out_shape=[pltpu.VMEM(by_head.shape, dtype), pltpu.HBM((TABLE_ROWS, owners), jnp.int32)],
        compiler_params=pltpu.CompilerParams(vmem_limit_bytes=PACK_LIMIT),
        name="pack",
    )(*map(in_hbm, (session_seat, cache_lens, old_slots, new_slots, kv_pool)))
    received = lax.all_to_all(
        outgoing.reshape(rows.shape), ("tp", "grp"), split_axis=0, concat_axis=0, tiled=True
    )

    leaving = pl.pallas_call(
        grow_kernel,
        in_specs=[smem, vmem, anywhere],
        out_specs=anywhere,
        scratch_shapes=[
            pltpu.VMEM((seats_group * spill, block_len, pair_width), dtype),
            pltpu.VMEM((seats_group, block_len, pair_width), dtype),
            pltpu.SemaphoreType.DMA,
            pltpu.SemaphoreType.DMA((seats_group,)),
        ],
        out_shape=pltpu.HBM(rows.shape, dtype),
        compiler_params=pltpu.CompilerParams(vmem_limit_bytes=GROW_LIMIT),
        name="grow",
    )(table, fresh, pltpu.with_memory_space_constraint(received, pltpu.VMEM))
    arrived = lax.all_to_all(leaving, ("tp", "grp"), split_axis=0, concat_axis=0, tiled=True)

    attention = pl.pallas_call(
        attend_kernel,
        in_specs=[smem, vmem, vmem, anywhere],
        out_specs=vmem,
        scratch_shapes=[
            pltpu.VMEM((seats_group, max_blocks * block_len, pair_width), dtype),
            pltpu.VMEM((2, turn, 2 * head_dim), jnp.float32),
            pltpu.VMEM((2, turn, head_dim), jnp.float32),
            pltpu.SemaphoreType.DMA((seats_group, max_blocks)),
        ],
        out_shape=jax.ShapeDtypeStruct(queries.shape, dtype),
        compiler_params=pltpu.CompilerParams(vmem_limit_bytes=ATTEND_LIMIT),
        cost_estimate=pl.CostEstimate(
            flops=4 * seats_group * heads * turn * max_blocks * block_len * head_dim,
            bytes_accessed=owners * block_len * pair_width * 2,
            transcendentals=seats_group * heads * turn * max_blocks * block_len,
        ),
        name="attend",
    )(table, in_hbm(queries), fresh, in_hbm(leaving))

    new_pool = pl.pallas_call(
        unpack_kernel,
        in_specs=[smem, anywhere],
        out_specs=anywhere,
        scratch_shapes=[
            pltpu.VMEM(blocks.shape, dtype),
            pltpu.VMEM(blocks.shape[1:], dtype),
            pltpu.SemaphoreType.DMA((group_count,)),
            pltpu.SemaphoreType.DMA((group_count,)),
        ],
        out_shape=blocks,
        compiler_params=pltpu.CompilerParams(vmem_limit_bytes=VMEM_LIMIT),
        name="unpack",
    )(table, arrived.reshape(by_head.shape))
    return attention, new_pool


def solution(mesh):
    in_specs = (
        P("grp", "tp", None, None),
        P("grp", "tp", None, None),
        P(("grp", "tp"), None, None, None),
        P(),
        P(),
        P(),
        P(),
    )
    out_specs = (P("grp", "tp", None, None), P(("grp", "tp"), None, None, None))
    return jax.shard_map(local, mesh=mesh, in_specs=in_specs, out_specs=out_specs, check_vma=False)
```

```python
import functools
import math

import jax
import jax.numpy as jnp
from jax import lax
from jax.experimental import pallas as pl
from jax.experimental.pallas import tpu as pltpu
from jax.sharding import PartitionSpec as P

MASKED = -1e30
CHUNK_BLOCKS = 8
PICK, TARGET, LENGTHS, EDGES, CODES, BLOCKS = range(6)
TABLE_ROWS = 8
VMEM_LIMIT = 60 * 1024 * 1024
PACK_LIMIT = 24 * 1024 * 1024
GROW_LIMIT = 24 * 1024 * 1024
ATTEND_LIMIT = 60 * 1024 * 1024


def pack_kernel(
    seat_ref, lens_ref, old_ref, new_ref, pool_ref, out_ref, table_ref, sems, *, seats, turn
):
    count, tp_count, block_len = pool_ref.shape[:3]
    groups = out_ref.shape[1]
    sessions, max_blocks = old_ref.shape
    owners = table_ref.shape[1]
    spill = turn // block_len + 1
    my_group = lax.axis_index("grp")
    first_slot = (my_group * tp_count + lax.axis_index("tp")) * count

    shape = (sessions, max_blocks)
    session = lax.broadcasted_iota(jnp.int32, shape, 0)
    block = lax.broadcasted_iota(jnp.int32, shape, 1)
    seat = jnp.zeros(shape, jnp.int32)
    length = jnp.zeros(shape, jnp.int32)
    for s in range(sessions):
        seat = jnp.where(session == s, seat_ref[s], seat)
        length = jnp.where(session == s, lens_ref[s], length)
    group = lax.div(seat, seats)

    def codes_of(slots, lengths):
        code = jnp.where(block * block_len < lengths, group + 1, 0)
        return [jnp.sum(jnp.where(slots - first_slot == i, code, 0)) for i in range(count)]

    old = old_ref[...]
    new = new_ref[...]

    def rank_of(slots):
        device = lax.div(slots, count)
        return lax.rem(device, tp_count) * groups + lax.div(device, tp_count)

    codes = codes_of(old, length)

    def copy(i):
        return pltpu.make_async_copy(pool_ref.at[i], out_ref.at[:, codes[i] - 1], sems.at[i])

    for i in range(count):
        pl.when(codes[i] > 0)(lambda i=i: copy(i).start())

    table_ref[...] = jnp.zeros_like(table_ref)
    lane = lax.broadcasted_iota(jnp.int32, (1, owners), 1)
    code_row = jnp.zeros((1, owners), jnp.int32)
    for i, code in enumerate(codes_of(new, length + turn)):
        code_row = jnp.where(lane == i, code, code_row)
    table_ref[CODES : CODES + 1, :] = code_row

    square = (max_blocks, max_blocks)
    diagonal = lax.broadcasted_iota(jnp.int32, square, 0) == lax.broadcasted_iota(jnp.int32, square, 1)
    owner = lax.broadcasted_iota(jnp.int32, (max_blocks, owners), 1)
    place = lax.broadcasted_iota(jnp.int32, (1, max_blocks), 1)
    pick_row = jnp.zeros((1, owners), jnp.int32)
    target_row = jnp.zeros((1, owners), jnp.int32)
    length_row = jnp.zeros((1, owners), jnp.int32)
    edge_row = jnp.zeros((1, owners), jnp.int32)
    for q in range(seats):
        mine = seat == my_group * seats + q

        def of_seat(values):
            return jnp.sum(jnp.where(mine, values, 0), axis=0, keepdims=True)

        def column(row):
            return jnp.sum(jnp.where(diagonal, row, 0), axis=1, keepdims=True)

        my_length = of_seat(length)
        source = of_seat(rank_of(old))
        past = place - lax.div(my_length, block_len)
        on_edge = jnp.logical_and(past >= 0, past < spill)
        pick = jnp.where(on_edge, owners + q * spill + past, source)
        from_owner = owner == column(source)
        pick_row += jnp.sum(jnp.where(from_owner, column(pick), 0), axis=0, keepdims=True)
        target = of_seat(rank_of(new))
        target_row += jnp.sum(jnp.where(from_owner, column(target), 0), axis=0, keepdims=True)
        edge = jnp.sum(jnp.where(past == 0, source, 0), axis=1, keepdims=True)
        edge_row = jnp.where(lane == q, edge, edge_row)
        length_row = jnp.where(lane == q, my_length[:, :1], length_row)
        table_ref[BLOCKS + q : BLOCKS + q + 1, :max_blocks] = target
    table_ref[PICK : PICK + 1, :] = pick_row
    table_ref[TARGET : TARGET + 1, :] = target_row
    table_ref[LENGTHS : LENGTHS + 1, :] = length_row
    table_ref[EDGES : EDGES + 1, :] = edge_row
    for i in range(count):
        pl.when(codes[i] > 0)(lambda i=i: copy(i).wait())


def unpack_kernel(table_ref, arrived_ref, cleared_ref, out_ref, held, load_sems, store_sems):
    count = out_ref.shape[0]

    def load(i):
        source = arrived_ref.at[:, table_ref[CODES, i] - 1]
        return pltpu.make_async_copy(source, held.at[i], load_sems.at[i])

    def store(i):
        return pltpu.make_async_copy(held.at[i], out_ref.at[i], store_sems.at[i])

    def forward(i):
        load(i).wait()
        store(i).start()

    for i in range(count):
        pl.when(table_ref[CODES, i] > 0)(lambda i=i: load(i).start())
    for i in range(count):
        pl.when(table_ref[CODES, i] > 0)(lambda i=i: forward(i))
    for i in range(count):
        pl.when(table_ref[CODES, i] > 0)(lambda i=i: store(i).wait())


def grow_kernel(
    table_ref, fresh_ref, recv_ref, out_ref, grown, edge_in, store_sem, edge_sems
):
    owners, block_len, width = recv_ref.shape
    seats, turn = fresh_ref.shape[:2]
    spill = turn // block_len + 1

    def edge_load(q):
        row = recv_ref.at[table_ref[EDGES, q]]
        return pltpu.make_async_copy(row, edge_in.at[q], edge_sems.at[q])

    def send(o, source):
        pltpu.make_async_copy(source, out_ref.at[table_ref[TARGET, o]], store_sem).start()

    for q in range(seats):
        edge_load(q).start()
    for o in range(owners):
        pl.when(table_ref[PICK, o] < owners)(lambda o=o: send(o, recv_ref.at[o]))
    row = lax.broadcasted_iota(jnp.int32, (block_len, width), 0)
    for q in range(seats):
        rest = lax.rem(table_ref[LENGTHS, q], block_len)
        tail = jnp.zeros((block_len, width), jnp.float32)
        moved = jnp.concatenate([fresh_ref[q].astype(jnp.float32), tail], axis=0)
        moved = pltpu.roll(moved, rest, 0)
        edge_load(q).wait()
        first = jnp.where(row < rest, edge_in[q].astype(jnp.float32), moved[:block_len])
        grown[q * spill] = first.astype(grown.dtype)
        for k in range(1, spill):
            later = moved[k * block_len : (k + 1) * block_len]
            grown[q * spill + k] = later.astype(grown.dtype)

    @pl.loop(0, owners)
    def _(o):
        pick = table_ref[PICK, o]
        pl.when(pick >= owners)(lambda: send(o, grown.at[pick - owners]))

    pltpu.make_async_copy(recv_ref, out_ref, store_sem).wait()


def attend_kernel(
    table_ref, queries_ref, fresh_ref, grown_ref, out_ref, cleared_ref,
    cache, acc, high, zeros, sems, clear_sems,
):
    seats = queries_ref.shape[0]
    block_len = grown_ref.shape[1]
    head_dim = queries_ref.shape[3]
    heads = queries_ref.shape[1]
    turn = queries_ref.shape[2]
    span = CHUNK_BLOCKS * block_len
    factor = head_dim ** (-0.5) * math.log2(math.e)
    pair = 2

    def row_copy(q, j):
        return pltpu.make_async_copy(
            grown_ref.at[table_ref[BLOCKS + q, j]],
            cache.at[q, pl.ds(pl.multiple_of(j * block_len, block_len), block_len)],
            sems.at[q, j],
        )

    def clear(i):
        return pltpu.make_async_copy(zeros, cleared_ref.at[i], clear_sems.at[i])

    def blocks_of(q):
        return (table_ref[LENGTHS, q] + block_len - 1) // block_len

    def chunks_of(q):
        return (table_ref[LENGTHS, q] + span - 1) // span

    for q in range(seats):
        pl.loop(0, blocks_of(q))(lambda j, q=q: row_copy(q, j).start())

    slots = cleared_ref.shape[0]
    zeros[...] = jnp.zeros_like(zeros)
    for i in range(slots):
        pl.when(table_ref[CODES, i] == 0)(lambda i=i: clear(i).start())

    def values_of(rows):
        ones = jnp.ones((rows.shape[0], head_dim), rows.dtype)
        return jnp.concatenate([rows[:, head_dim:], ones], axis=1)

    def score(query, rows):
        return (
            lax.dot_general(
                query, rows[:, :head_dim], (((1,), (1,)), ((), ())),
                preferred_element_type=jnp.float32,
            )
            * factor
        )

    def weigh(scores, top, rows):
        weights = jnp.exp2(scores - top).astype(jnp.bfloat16)
        return jnp.dot(weights, values_of(rows), preferred_element_type=jnp.float32)

    for q in range(seats):
        length = table_ref[LENGTHS, q]
        pl.loop(0, blocks_of(q))(lambda j, q=q: row_copy(q, j).wait())

        @pl.loop(blocks_of(q), chunks_of(q) * CHUNK_BLOCKS)
        def _(j, q=q):
            start = pl.multiple_of(j * block_len, block_len)
            cache[q, pl.ds(start, block_len)] = jnp.zeros((block_len, cache.shape[2]), cache.dtype)

        @pl.loop(0, heads // pair)
        def _(h, q=q, length=length):
            row = lax.broadcasted_iota(jnp.int32, (turn, turn), 0)
            column = lax.broadcasted_iota(jnp.int32, (turn, turn), 1)
            fresh = fresh_ref[q]
            for k in range(pair):
                scores = score(queries_ref[q, h * pair + k], fresh)
                scores = jnp.where(column <= row, scores, MASKED)
                top = jnp.max(scores, axis=1, keepdims=True)
                acc[k] = weigh(scores, top, fresh)
                high[k] = jnp.broadcast_to(top, high.shape[1:])

            def step(c, masked):
                start = pl.multiple_of(c * span, span)
                rows = cache[q, pl.ds(start, span)]
                for k in range(pair):
                    scores = score(queries_ref[q, h * pair + k], rows)
                    if masked:
                        position = start + lax.broadcasted_iota(jnp.int32, (1, span), 1)
                        scores = jnp.where(position < length, scores, MASKED)
                    old = high[k, :, :1]
                    top = jnp.maximum(old, jnp.max(scores, axis=1, keepdims=True))
                    acc[k] = acc[k] * jnp.exp2(old - top) + weigh(scores, top, rows)
                    high[k] = jnp.broadcast_to(top, high.shape[1:])

            full = length // span
            pl.loop(0, full)(lambda c: step(c, False))
            pl.when(length > full * span)(lambda: step(full, True))
            for k in range(pair):
                total = acc[k, :, head_dim : head_dim + 1]
                out_ref[q, h * pair + k] = (acc[k, :, :head_dim] / total).astype(out_ref.dtype)

    for i in range(slots):
        pl.when(table_ref[CODES, i] == 0)(lambda i=i: clear(i).wait())


def local(queries, new_kv, kv_pool, cache_lens, session_seat, old_slots, new_slots):
    group_count = lax.axis_size("grp")
    tp_count = lax.axis_size("tp")
    pool_dev, kv_heads, block_len, pair_width = kv_pool.shape
    seats_group, heads, turn, head_dim = queries.shape
    max_blocks = old_slots.shape[1]
    owners = group_count * tp_count
    assert pool_dev == group_count and kv_heads == tp_count and max_blocks <= owners
    dtype = kv_pool.dtype
    in_hbm = functools.partial(pltpu.with_memory_space_constraint, memory_space=pltpu.HBM)
    anywhere = pl.BlockSpec(memory_space=pl.ANY)
    vmem = pl.BlockSpec(memory_space=pltpu.VMEM)
    smem = pl.BlockSpec(memory_space=pltpu.SMEM)
    rows = jax.ShapeDtypeStruct((owners, block_len, pair_width), dtype)
    blocks = jax.ShapeDtypeStruct((group_count, kv_heads, block_len, pair_width), dtype)
    by_head = jax.ShapeDtypeStruct((kv_heads, group_count, block_len, pair_width), dtype)
    fresh = new_kv.reshape(seats_group, turn, pair_width)
    spill = turn // block_len + 1

    outgoing, table = pl.pallas_call(
        functools.partial(pack_kernel, seats=seats_group, turn=turn),
        in_specs=[smem, smem, vmem, vmem, anywhere],
        out_specs=[anywhere, vmem],
        scratch_shapes=[pltpu.SemaphoreType.DMA((group_count,))],
        out_shape=[pltpu.VMEM(by_head.shape, dtype), pltpu.HBM((TABLE_ROWS, owners), jnp.int32)],
        compiler_params=pltpu.CompilerParams(vmem_limit_bytes=PACK_LIMIT),
        name="pack",
    )(*map(in_hbm, (session_seat, cache_lens, old_slots, new_slots, kv_pool)))
    received = lax.all_to_all(
        outgoing.reshape(rows.shape), ("tp", "grp"), split_axis=0, concat_axis=0, tiled=True
    )

    leaving = pl.pallas_call(
        grow_kernel,
        in_specs=[smem, vmem, anywhere],
        out_specs=anywhere,
        scratch_shapes=[
            pltpu.VMEM((seats_group * spill, block_len, pair_width), dtype),
            pltpu.VMEM((seats_group, block_len, pair_width), dtype),
            pltpu.SemaphoreType.DMA,
            pltpu.SemaphoreType.DMA((seats_group,)),
        ],
        out_shape=pltpu.HBM(rows.shape, dtype),
        compiler_params=pltpu.CompilerParams(vmem_limit_bytes=GROW_LIMIT),
        name="grow",
    )(table, fresh, pltpu.with_memory_space_constraint(received, pltpu.VMEM))
    arrived = lax.all_to_all(leaving, ("tp", "grp"), split_axis=0, concat_axis=0, tiled=True)

    attention, cleared = pl.pallas_call(
        attend_kernel,
        in_specs=[smem, vmem, vmem, anywhere],
        out_specs=[vmem, anywhere],
        scratch_shapes=[
            pltpu.VMEM((seats_group, max_blocks * block_len, pair_width), dtype),
            pltpu.VMEM((2, turn, 2 * head_dim), jnp.float32),
            pltpu.VMEM((2, turn, head_dim), jnp.float32),
            pltpu.VMEM(blocks.shape[1:], dtype),
            pltpu.SemaphoreType.DMA((seats_group, max_blocks)),
            pltpu.SemaphoreType.DMA((group_count,)),
        ],
        out_shape=[jax.ShapeDtypeStruct(queries.shape, dtype), pltpu.HBM(blocks.shape, dtype)],
        compiler_params=pltpu.CompilerParams(vmem_limit_bytes=ATTEND_LIMIT),
        cost_estimate=pl.CostEstimate(
            flops=4 * seats_group * heads * turn * max_blocks * block_len * head_dim,
            bytes_accessed=owners * block_len * pair_width * 2,
            transcendentals=seats_group * heads * turn * max_blocks * block_len,
        ),
        name="attend",
    )(table, in_hbm(queries), fresh, in_hbm(leaving))

    new_pool = pl.pallas_call(
        unpack_kernel,
        in_specs=[smem, anywhere, anywhere],
        out_specs=anywhere,
        scratch_shapes=[
            pltpu.VMEM(blocks.shape, dtype),
            pltpu.SemaphoreType.DMA((group_count,)),
            pltpu.SemaphoreType.DMA((group_count,)),
        ],
        out_shape=blocks,
        compiler_params=pltpu.CompilerParams(vmem_limit_bytes=VMEM_LIMIT),
        input_output_aliases={2: 0},
        name="unpack",
    )(table, arrived.reshape(by_head.shape), cleared)
    return attention, new_pool


def solution(mesh):
    in_specs = (
        P("grp", "tp", None, None),
        P("grp", "tp", None, None),
        P(("grp", "tp"), None, None, None),
        P(),
        P(),
        P(),
        P(),
    )
    out_specs = (P("grp", "tp", None, None), P(("grp", "tp"), None, None, None))
    return jax.shard_map(local, mesh=mesh, in_specs=in_specs, out_specs=out_specs, check_vma=False)
```

```python
import functools
import math

import jax
import jax.numpy as jnp
from jax import lax
from jax.experimental import pallas as pl
from jax.experimental.pallas import tpu as pltpu
from jax.sharding import PartitionSpec as P

MASKED = -1e30
CHUNK_BLOCKS = 8
PICK, TARGET, LENGTHS, EDGES, CODES, BLOCKS = range(6)
TABLE_ROWS = 8
VMEM_LIMIT = 60 * 1024 * 1024
PACK_LIMIT = 24 * 1024 * 1024
GROW_LIMIT = 24 * 1024 * 1024
ATTEND_LIMIT = 60 * 1024 * 1024


def pack_kernel(
    seat_ref, lens_ref, old_ref, new_ref, pool_ref, out_ref, table_ref, sems, *, seats, turn
):
    count, tp_count, block_len = pool_ref.shape[:3]
    groups = out_ref.shape[1]
    sessions, max_blocks = old_ref.shape
    owners = table_ref.shape[1]
    spill = turn // block_len + 1
    my_group = lax.axis_index("grp")
    first_slot = (my_group * tp_count + lax.axis_index("tp")) * count

    shape = (sessions, max_blocks)
    session = lax.broadcasted_iota(jnp.int32, shape, 0)
    block = lax.broadcasted_iota(jnp.int32, shape, 1)
    seat = jnp.zeros(shape, jnp.int32)
    length = jnp.zeros(shape, jnp.int32)
    for s in range(sessions):
        seat = jnp.where(session == s, seat_ref[s], seat)
        length = jnp.where(session == s, lens_ref[s], length)
    group = lax.div(seat, seats)

    def codes_of(slots, lengths):
        code = jnp.where(block * block_len < lengths, group + 1, 0)
        return [jnp.sum(jnp.where(slots - first_slot == i, code, 0)) for i in range(count)]

    old = old_ref[...]
    new = new_ref[...]

    def rank_of(slots):
        device = lax.div(slots, count)
        return lax.rem(device, tp_count) * groups + lax.div(device, tp_count)

    codes = codes_of(old, length)

    def copy(i):
        return pltpu.make_async_copy(pool_ref.at[i], out_ref.at[:, codes[i] - 1], sems.at[i])

    for i in range(count):
        pl.when(codes[i] > 0)(lambda i=i: copy(i).start())

    table_ref[...] = jnp.zeros_like(table_ref)
    lane = lax.broadcasted_iota(jnp.int32, (1, owners), 1)
    code_row = jnp.zeros((1, owners), jnp.int32)
    for i, code in enumerate(codes_of(new, length + turn)):
        code_row = jnp.where(lane == i, code, code_row)
    table_ref[CODES : CODES + 1, :] = code_row

    square = (max_blocks, max_blocks)
    diagonal = lax.broadcasted_iota(jnp.int32, square, 0) == lax.broadcasted_iota(jnp.int32, square, 1)
    owner = lax.broadcasted_iota(jnp.int32, (max_blocks, owners), 1)
    place = lax.broadcasted_iota(jnp.int32, (1, max_blocks), 1)
    pick_row = jnp.zeros((1, owners), jnp.int32)
    target_row = jnp.zeros((1, owners), jnp.int32)
    length_row = jnp.zeros((1, owners), jnp.int32)
    edge_row = jnp.zeros((1, owners), jnp.int32)
    for q in range(seats):
        mine = seat == my_group * seats + q

        def of_seat(values):
            return jnp.sum(jnp.where(mine, values, 0), axis=0, keepdims=True)

        def column(row):
            return jnp.sum(jnp.where(diagonal, row, 0), axis=1, keepdims=True)

        my_length = of_seat(length)
        source = of_seat(rank_of(old))
        past = place - lax.div(my_length, block_len)
        on_edge = jnp.logical_and(past >= 0, past < spill)
        pick = jnp.where(on_edge, owners + q * spill + past, source)
        from_owner = owner == column(source)
        pick_row += jnp.sum(jnp.where(from_owner, column(pick), 0), axis=0, keepdims=True)
        target = of_seat(rank_of(new))
        target_row += jnp.sum(jnp.where(from_owner, column(target), 0), axis=0, keepdims=True)
        edge = jnp.sum(jnp.where(past == 0, source, 0), axis=1, keepdims=True)
        edge_row = jnp.where(lane == q, edge, edge_row)
        length_row = jnp.where(lane == q, my_length[:, :1], length_row)
        table_ref[BLOCKS + q : BLOCKS + q + 1, :max_blocks] = target
    table_ref[PICK : PICK + 1, :] = pick_row
    table_ref[TARGET : TARGET + 1, :] = target_row
    table_ref[LENGTHS : LENGTHS + 1, :] = length_row
    table_ref[EDGES : EDGES + 1, :] = edge_row
    for i in range(count):
        pl.when(codes[i] > 0)(lambda i=i: copy(i).wait())


def unpack_kernel(table_ref, arrived_ref, cleared_ref, out_ref, held, load_sems, store_sems):
    count, parts = load_sems.shape
    share = held.shape[1] // parts
    pieces = [(i, pl.ds(k * share, share), k) for k in range(parts) for i in range(count)]

    def load(i, heads, k):
        source = arrived_ref.at[heads, table_ref[CODES, i] - 1]
        return pltpu.make_async_copy(source, held.at[i, heads], load_sems.at[i, k])

    def store(i, heads, k):
        return pltpu.make_async_copy(held.at[i, heads], out_ref.at[i, heads], store_sems.at[i, k])

    def forward(piece):
        load(*piece).wait()
        store(*piece).start()

    for piece in pieces:
        pl.when(table_ref[CODES, piece[0]] > 0)(lambda piece=piece: load(*piece).start())
    for piece in pieces:
        pl.when(table_ref[CODES, piece[0]] > 0)(lambda piece=piece: forward(piece))
    for piece in pieces:
        pl.when(table_ref[CODES, piece[0]] > 0)(lambda piece=piece: store(*piece).wait())


def grow_kernel(
    table_ref, fresh_ref, recv_ref, out_ref, grown, edge_in, store_sem, edge_sems
):
    owners, block_len, width = recv_ref.shape
    seats, turn = fresh_ref.shape[:2]
    spill = turn // block_len + 1

    def edge_load(q):
        row = recv_ref.at[table_ref[EDGES, q]]
        return pltpu.make_async_copy(row, edge_in.at[q], edge_sems.at[q])

    def send(o, source):
        pltpu.make_async_copy(source, out_ref.at[table_ref[TARGET, o]], store_sem).start()

    for q in range(seats):
        edge_load(q).start()
    for o in range(owners):
        pl.when(table_ref[PICK, o] < owners)(lambda o=o: send(o, recv_ref.at[o]))
    row = lax.broadcasted_iota(jnp.int32, (block_len, width), 0)
    for q in range(seats):
        rest = lax.rem(table_ref[LENGTHS, q], block_len)
        tail = jnp.zeros((block_len, width), jnp.float32)
        moved = jnp.concatenate([fresh_ref[q].astype(jnp.float32), tail], axis=0)
        moved = pltpu.roll(moved, rest, 0)
        edge_load(q).wait()
        first = jnp.where(row < rest, edge_in[q].astype(jnp.float32), moved[:block_len])
        grown[q * spill] = first.astype(grown.dtype)
        for k in range(1, spill):
            later = moved[k * block_len : (k + 1) * block_len]
            grown[q * spill + k] = later.astype(grown.dtype)

    @pl.loop(0, owners)
    def _(o):
        pick = table_ref[PICK, o]
        pl.when(pick >= owners)(lambda: send(o, grown.at[pick - owners]))

    pltpu.make_async_copy(recv_ref, out_ref, store_sem).wait()


def attend_kernel(
    table_ref, queries_ref, fresh_ref, grown_ref, out_ref, cleared_ref,
    cache, acc, high, zeros, sems, clear_sems,
):
    seats = queries_ref.shape[0]
    block_len = grown_ref.shape[1]
    head_dim = queries_ref.shape[3]
    heads = queries_ref.shape[1]
    turn = queries_ref.shape[2]
    span = CHUNK_BLOCKS * block_len
    factor = head_dim ** (-0.5) * math.log2(math.e)
    pair = 2

    def row_copy(q, j):
        return pltpu.make_async_copy(
            grown_ref.at[table_ref[BLOCKS + q, j]],
            cache.at[q, pl.ds(pl.multiple_of(j * block_len, block_len), block_len)],
            sems.at[q, j],
        )

    def clear(i):
        return pltpu.make_async_copy(zeros, cleared_ref.at[i], clear_sems.at[i])

    def blocks_of(q):
        return (table_ref[LENGTHS, q] + block_len - 1) // block_len

    def chunks_of(q):
        return (table_ref[LENGTHS, q] + span - 1) // span

    for q in range(seats):
        pl.loop(0, blocks_of(q))(lambda j, q=q: row_copy(q, j).start())

    slots = cleared_ref.shape[0]
    zeros[...] = jnp.zeros_like(zeros)
    for i in range(slots):
        pl.when(table_ref[CODES, i] == 0)(lambda i=i: clear(i).start())

    def values_of(rows):
        ones = jnp.ones((rows.shape[0], head_dim), rows.dtype)
        return jnp.concatenate([rows[:, head_dim:], ones], axis=1)

    def score(query, rows):
        return (
            lax.dot_general(
                query, rows[:, :head_dim], (((1,), (1,)), ((), ())),
                preferred_element_type=jnp.float32,
            )
            * factor
        )

    def weigh(scores, top, rows):
        weights = jnp.exp2(scores - top).astype(jnp.bfloat16)
        return jnp.dot(weights, values_of(rows), preferred_element_type=jnp.float32)

    for q in range(seats):
        length = table_ref[LENGTHS, q]
        pl.loop(0, blocks_of(q))(lambda j, q=q: row_copy(q, j).wait())

        @pl.loop(blocks_of(q), chunks_of(q) * CHUNK_BLOCKS)
        def _(j, q=q):
            start = pl.multiple_of(j * block_len, block_len)
            cache[q, pl.ds(start, block_len)] = jnp.zeros((block_len, cache.shape[2]), cache.dtype)

        @pl.loop(0, heads // pair)
        def _(h, q=q, length=length):
            row = lax.broadcasted_iota(jnp.int32, (turn, turn), 0)
            column = lax.broadcasted_iota(jnp.int32, (turn, turn), 1)
            fresh = fresh_ref[q]
            for k in range(pair):
                scores = score(queries_ref[q, h * pair + k], fresh)
                scores = jnp.where(column <= row, scores, MASKED)
                top = jnp.max(scores, axis=1, keepdims=True)
                acc[k] = weigh(scores, top, fresh)
                high[k] = jnp.broadcast_to(top, high.shape[1:])

            def step(c, masked):
                start = pl.multiple_of(c * span, span)
                rows = cache[q, pl.ds(start, span)]
                for k in range(pair):
                    scores = score(queries_ref[q, h * pair + k], rows)
                    if masked:
                        position = start + lax.broadcasted_iota(jnp.int32, (1, span), 1)
                        scores = jnp.where(position < length, scores, MASKED)
                    old = high[k, :, :1]
                    top = jnp.maximum(old, jnp.max(scores, axis=1, keepdims=True))
                    acc[k] = acc[k] * jnp.exp2(old - top) + weigh(scores, top, rows)
                    high[k] = jnp.broadcast_to(top, high.shape[1:])

            full = length // span
            pl.loop(0, full)(lambda c: step(c, False))
            pl.when(length > full * span)(lambda: step(full, True))
            for k in range(pair):
                total = acc[k, :, head_dim : head_dim + 1]
                out_ref[q, h * pair + k] = (acc[k, :, :head_dim] / total).astype(out_ref.dtype)

    for i in range(slots):
        pl.when(table_ref[CODES, i] == 0)(lambda i=i: clear(i).wait())


def local(queries, new_kv, kv_pool, cache_lens, session_seat, old_slots, new_slots):
    group_count = lax.axis_size("grp")
    tp_count = lax.axis_size("tp")
    pool_dev, kv_heads, block_len, pair_width = kv_pool.shape
    seats_group, heads, turn, head_dim = queries.shape
    max_blocks = old_slots.shape[1]
    owners = group_count * tp_count
    assert pool_dev == group_count and kv_heads == tp_count and max_blocks <= owners
    dtype = kv_pool.dtype
    in_hbm = functools.partial(pltpu.with_memory_space_constraint, memory_space=pltpu.HBM)
    anywhere = pl.BlockSpec(memory_space=pl.ANY)
    vmem = pl.BlockSpec(memory_space=pltpu.VMEM)
    smem = pl.BlockSpec(memory_space=pltpu.SMEM)
    rows = jax.ShapeDtypeStruct((owners, block_len, pair_width), dtype)
    blocks = jax.ShapeDtypeStruct((group_count, kv_heads, block_len, pair_width), dtype)
    by_head = jax.ShapeDtypeStruct((kv_heads, group_count, block_len, pair_width), dtype)
    fresh = new_kv.reshape(seats_group, turn, pair_width)
    spill = turn // block_len + 1

    outgoing, table = pl.pallas_call(
        functools.partial(pack_kernel, seats=seats_group, turn=turn),
        in_specs=[smem, smem, vmem, vmem, anywhere],
        out_specs=[anywhere, vmem],
        scratch_shapes=[pltpu.SemaphoreType.DMA((group_count,))],
        out_shape=[pltpu.VMEM(by_head.shape, dtype), pltpu.HBM((TABLE_ROWS, owners), jnp.int32)],
        compiler_params=pltpu.CompilerParams(vmem_limit_bytes=PACK_LIMIT),
        name="pack",
    )(*map(in_hbm, (session_seat, cache_lens, old_slots, new_slots, kv_pool)))
    received = lax.all_to_all(
        outgoing.reshape(rows.shape), ("tp", "grp"), split_axis=0, concat_axis=0, tiled=True
    )

    leaving = pl.pallas_call(
        grow_kernel,
        in_specs=[smem, vmem, anywhere],
        out_specs=anywhere,
        scratch_shapes=[
            pltpu.VMEM((seats_group * spill, block_len, pair_width), dtype),
            pltpu.VMEM((seats_group, block_len, pair_width), dtype),
            pltpu.SemaphoreType.DMA,
            pltpu.SemaphoreType.DMA((seats_group,)),
        ],
        out_shape=pltpu.HBM(rows.shape, dtype),
        compiler_params=pltpu.CompilerParams(vmem_limit_bytes=GROW_LIMIT),
        name="grow",
    )(table, fresh, pltpu.with_memory_space_constraint(received, pltpu.VMEM))
    arrived = lax.all_to_all(leaving, ("tp", "grp"), split_axis=0, concat_axis=0, tiled=True)

    attention, cleared = pl.pallas_call(
        attend_kernel,
        in_specs=[smem, vmem, vmem, anywhere],
        out_specs=[vmem, anywhere],
        scratch_shapes=[
            pltpu.VMEM((seats_group, max_blocks * block_len, pair_width), dtype),
            pltpu.VMEM((2, turn, 2 * head_dim), jnp.float32),
            pltpu.VMEM((2, turn, head_dim), jnp.float32),
            pltpu.VMEM(blocks.shape[1:], dtype),
            pltpu.SemaphoreType.DMA((seats_group, max_blocks)),
            pltpu.SemaphoreType.DMA((group_count,)),
        ],
        out_shape=[jax.ShapeDtypeStruct(queries.shape, dtype), pltpu.HBM(blocks.shape, dtype)],
        compiler_params=pltpu.CompilerParams(vmem_limit_bytes=ATTEND_LIMIT),
        cost_estimate=pl.CostEstimate(
            flops=4 * seats_group * heads * turn * max_blocks * block_len * head_dim,
            bytes_accessed=owners * block_len * pair_width * 2,
            transcendentals=seats_group * heads * turn * max_blocks * block_len,
        ),
        name="attend",
    )(table, in_hbm(queries), fresh, in_hbm(leaving))

    new_pool = pl.pallas_call(
        unpack_kernel,
        in_specs=[smem, anywhere, anywhere],
        out_specs=anywhere,
        scratch_shapes=[
            pltpu.VMEM(blocks.shape, dtype),
            pltpu.SemaphoreType.DMA((group_count, math.gcd(kv_heads, 4))),
            pltpu.SemaphoreType.DMA((group_count, math.gcd(kv_heads, 4))),
        ],
        out_shape=blocks,
        compiler_params=pltpu.CompilerParams(vmem_limit_bytes=VMEM_LIMIT),
        input_output_aliases={2: 0},
        name="unpack",
    )(table, arrived.reshape(by_head.shape), cleared)
    return attention, new_pool


def solution(mesh):
    in_specs = (
        P("grp", "tp", None, None),
        P("grp", "tp", None, None),
        P(("grp", "tp"), None, None, None),
        P(),
        P(),
        P(),
        P(),
    )
    out_specs = (P("grp", "tp", None, None), P(("grp", "tp"), None, None, None))
    return jax.shard_map(local, mesh=mesh, in_specs=in_specs, out_specs=out_specs, check_vma=False)
```
